128 devices in a mesh: row: 32 (over y, x, core), col: 4 (over z).
Axes of the slice: x: 4, y: 4, z: 4, core: 2. Of those that a mesh axis runs over, the one named last changes fastest.
Arguments:
- probe_signs: int32 [32, 8, 1024, 1024], P(None, None, 'row', 'col'), may hold values from 0 to 1
- prior_scale: float32 [8, 1024, 1024], P(None, 'row', 'col'), may hold values from 0.02 to 6
- prior_factor: float32 [8, 8], replicated, may hold values from -3 to 3
- band_mix: float32 [8, 8], replicated, may hold values from -3 to 3
- inverse_noise_variance: float32 [8, 1024, 1024], P(None, 'row', 'col'), may hold values from 0.1 to 1
Outputs:
- basis: float32 [32, 8, 1024, 1024], P(None, None, 'row', 'col')
- r_factor: float32 [32, 32], replicated
The draws below stay inside these ranges and needn't reach their ends.
All inputs are finite; a program needn't handle non-finite values.
Results may differ from the reference program's by a relative error of at most 0.00022.
Values sent between devices are 32-bit elements; how exact they have to be, the bound alone decides.
No kernel may reach another device: no remote copies, remote signals or barrier semaphores. Data moves between devices by JAX's collectives and lax.ppermute only.
A program may use at most 256 MiB of HBM per device.

```python
import math
import jax
import jax.numpy as jnp
from jax import lax

BANDS = 8
PROBES = 32
TAPS = 31
HALF = 15
NR = 1024
NC = 1024


def draw_prior_scale(key, part):
    key = jax.random.fold_in(key, 11)
    subkeys = jax.random.split(key, 5)
    return jnp.exp(jax.random.uniform(subkeys[4], (BANDS, NR, NC), jnp.float32, math.log(0.3), math.log(3.0)))


def draw_prior_factor(key, part):
    key = jax.random.fold_in(key, 12)
    subkeys = jax.random.split(key, 5)
    values = jnp.clip(jax.random.normal(subkeys[4], (BANDS, BANDS), jnp.float32), -6.0, 6.0)
    return values / math.sqrt(BANDS)


def draw_band_mix(key, part):
    key = jax.random.fold_in(key, 13)
    subkeys = jax.random.split(key, 5)
    values = jnp.clip(jax.random.normal(subkeys[4], (BANDS, BANDS), jnp.float32), -6.0, 6.0)
    return values / math.sqrt(BANDS)


def set_ends(values, key, smallest, largest):
    spot = [jax.random.randint(jax.random.fold_in(key, axis), (), 0, length) for axis, length in enumerate(values.shape)]
    longest = values.shape.index(max(values.shape))
    beside = spot[:longest] + [(spot[longest] + 1) % values.shape[longest]] + spot[longest + 1:]
    return values.at[tuple(spot)].set(smallest).at[tuple(beside)].set(largest)


def block_levels(rng, dims, cuts, low, high):
    def one(dim, parts):
        steps = jax.random.uniform(jax.random.fold_in(jax.random.fold_in(rng, 6), dim), (parts,), jnp.float32, low / len(cuts), high / len(cuts))
        return jnp.repeat(jnp.exp(steps), dims[dim] // parts).reshape((-1,) + (1,) * (len(dims) - dim - 1))

    loudness = one(*cuts[0])
    for cut in cuts[1:]:
        loudness = loudness * one(*cut)
    return loudness


def setup_inputs(seed: int = 0) -> dict:
    key_of = jax.random.split(jax.random.key(seed), 6)
    probe_signs = set_ends(jax.random.randint(key_of[0], (PROBES, BANDS, NR, NC), 0, 2), jax.random.fold_in(key_of[0], 1), 0, 1).astype(jnp.int32)
    prior_scale = draw_prior_scale(jax.random.fold_in(key_of[5], 71), 0)
    prior_factor = draw_prior_factor(jax.random.fold_in(key_of[5], 71), 0)
    band_mix = draw_band_mix(jax.random.fold_in(key_of[5], 71), 0)
    inverse_noise_variance = jnp.clip(jnp.exp(math.log(1.0) - 2.3025851 * jax.random.uniform(key_of[4], (BANDS, NR, NC), jnp.float32) ** block_levels(key_of[4], (BANDS, NR, NC), ((1, 32), (2, 4)), -0.2, 0.2)), 0.1, 1.0)
    return dict(probe_signs=probe_signs, prior_scale=prior_scale, prior_factor=prior_factor, band_mix=band_mix, inverse_noise_variance=inverse_noise_variance)


def tap_weights():
    offsets = jnp.arange(TAPS, dtype=jnp.float32) - HALF
    sigma = 1.0 + 0.5 * jnp.arange(BANDS, dtype=jnp.float32)
    raw = jnp.exp(-offsets[None, :] ** 2 / (2.0 * sigma[:, None] ** 2))
    return raw / lax.optimization_barrier(jnp.sum(raw, axis=1, keepdims=True))

def blur(image_plane, taps):
    rows_all = image_plane.shape[1]
    cols_all = image_plane.shape[2]
    padded = jnp.pad(image_plane, ((0, 0), (HALF, HALF), (0, 0)))
    along_rows = jnp.zeros_like(image_plane)
    for shift in range(TAPS):
        along_rows = along_rows + taps[:, shift, None, None] * padded[:, shift:shift + rows_all, :]
    padded = jnp.pad(along_rows, ((0, 0), (0, 0), (HALF, HALF)))
    result = jnp.zeros_like(image_plane)
    for shift in range(TAPS):
        result = result + taps[:, shift, None, None] * padded[:, :, shift:shift + cols_all]
    return result

def mix_bands(dense_matrix, image_plane):
    return jnp.einsum('bc,crs->brs', dense_matrix, image_plane, precision=lax.Precision.HIGHEST)

def reference(probe_signs, prior_scale, prior_factor, band_mix, inverse_noise_variance):
    taps = tap_weights()

    def one_probe(signs):
        sign = 2.0 * signs.astype(jnp.float32) - 1.0
        shaped = mix_bands(prior_factor, prior_scale * sign)
        blurred_image = blur(shaped, taps)
        weighted = inverse_noise_variance * mix_bands(band_mix, blurred_image)
        back = mix_bands(band_mix.T, weighted)
        back = blur(back, taps)
        return prior_scale * mix_bands(prior_factor.T, back) + sign
    sketch = lax.map(one_probe, probe_signs)
    dense_matrix = sketch.reshape(PROBES, -1)
    hi = lax.Precision.HIGHEST
    gram_one = jnp.dot(dense_matrix, dense_matrix.T, precision=hi)
    lower_one = jnp.linalg.cholesky(gram_one)
    first = jax.scipy.linalg.solve_triangular(lower_one, dense_matrix, lower=True)
    gram_two = jnp.dot(first, first.T, precision=hi)
    lower_two = jnp.linalg.cholesky(gram_two)
    latter_part = jax.scipy.linalg.solve_triangular(lower_two, first, lower=True)
    factor = jnp.dot(lower_one, lower_two, precision=hi).T
    total_rows = jnp.float32(dense_matrix.shape[1])
    basis = (latter_part * jnp.sqrt(total_rows)).reshape(sketch.shape)
    return (basis, factor / jnp.sqrt(total_rows))
```

```python
import numpy as np
import jax
import jax.numpy as jnp
from jax import lax
from jax.experimental import pallas as pl
from jax.experimental.pallas import tpu as pltpu
from jax.sharding import PartitionSpec as P

BANDS = 8
HALF = 15
TAPS = 31
ROWS = 32
COLS = 256
CHUNKS = 4
F32 = jnp.float32
BF16 = jnp.bfloat16
HI = lax.Precision.HIGHEST
VMEM = pl.BlockSpec(memory_space=pltpu.VMEM)


def taps_np():
    offsets = np.arange(TAPS) - HALF
    sigma = 1.0 + 0.5 * np.arange(BANDS)
    raw = np.exp(-offsets[None, :] ** 2 / (2.0 * sigma[:, None] ** 2))
    return raw / raw.sum(axis=1, keepdims=True)


def table_np(pos_in, pos_out):
    taps = taps_np()
    offset = np.asarray(pos_in)[:, None] - np.asarray(pos_out)[None, :]
    inside = np.abs(offset) <= HALF
    return np.where(inside[None], taps[:, np.clip(offset + HALF, 0, TAPS - 1)], 0.0)


def split_np(values):
    high = values.astype(BF16)
    low = (values - high.astype(np.float64)).astype(BF16)
    return high, low


def row_constants():
    out = np.arange(ROWS)
    main = table_np(np.arange(ROWS), out)
    above = table_np(np.arange(-HALF, 0), out)
    below = table_np(np.arange(ROWS, ROWS + HALF), out)
    by_out = np.zeros((BANDS, ROWS, 512))
    by_in = np.zeros((BANDS, ROWS, 512))
    pick = np.zeros((BANDS, 512))
    for c in range(BANDS):
        parts = ((c * ROWS, ROWS, main), (256 + c * HALF, HALF, above), (376 + c * HALF, HALF, below))
        for start, size, table in parts:
            by_out[:, :, start:start + size] = table.transpose(0, 2, 1)
            by_in[:, :, start:start + size] = table[c].T[None]
            pick[c, start:start + size] = 1.0
    spread = np.repeat(np.eye(BANDS), ROWS, axis=0)
    same = np.tile(np.eye(ROWS), (BANDS, BANDS))
    return [v.astype(np.float32) for v in (by_out.reshape(256, 512), by_in.reshape(256, 512), pick, spread, same)]


def col_constants():
    out = np.arange(COLS)
    main = table_np(np.arange(COLS), out)
    left = table_np(np.arange(-16, 0), out)
    right = table_np(np.arange(COLS, COLS + 16), out)
    halo = np.zeros((BANDS, 256, COLS))
    for b in range(BANDS):
        halo[b, 16 * b:16 * b + 16] = left[b]
        halo[b, 128 + 16 * b:128 + 16 * b + 16] = right[b]
    return split_np(main) + split_np(halo)


def split(values):
    high = values.astype(BF16)
    return high, (values - high.astype(F32)).astype(BF16)


def dot(a, b, precision=None):
    return lax.dot_general(a, b, (((1,), (0,)), ((), ())), precision=precision, preferred_element_type=F32)


def dot_nt(a, b):
    return lax.dot_general(a, b, (((1,), (1,)), ((), ())), preferred_element_type=F32)


def stacked(values):
    high, low = split(values)
    return jnp.concatenate([high, high, low], axis=0)


def params(mib=40):
    return pltpu.CompilerParams(vmem_limit_bytes=mib * 2**20)


def cost(flops, moved):
    return pl.CostEstimate(flops=int(flops), bytes_accessed=int(moved), transcendentals=0)


def prepare_kernel(factor, mix, by_out, by_in, pick, spread, same, first_m, last_m, mix_m, back_m):
    def expand(small, right):
        return dot(dot(spread[...], small, HI), right, HI)

    def store(out, whole):
        for part in range(whole.shape[1] // 256):
            high, low = split(whole[:, part * 256:part * 256 + 256])
            out[:, part * 768:part * 768 + 256] = high
            out[:, part * 768 + 256:part * 768 + 512] = low
            out[:, part * 768 + 512:part * 768 + 768] = high

    f = factor[...]
    a = mix[...]
    store(first_m, expand(f, pick[...]) * by_out[...])
    store(last_m, expand(f.T, pick[...]) * by_in[...])
    store(mix_m, expand(a, pick[:, :256]) * same[...])
    store(back_m, expand(a.T, pick[:, :256]) * same[...])


def prepare(factor, mix):
    wide = jax.ShapeDtypeStruct((256, 1536), BF16)
    narrow = jax.ShapeDtypeStruct((256, 768), BF16)
    return pl.pallas_call(
        prepare_kernel, out_shape=(wide, wide, narrow, narrow),
        in_specs=[VMEM] * 7, out_specs=(VMEM,) * 4, compiler_params=params(),
        name="prepare",
    )(factor, mix, *[jnp.asarray(v) for v in row_constants()])


def signed(ref_value):
    return 2.0 * ref_value.astype(F32) - 1.0


def store_edges(tile, top, bottom, p):
    for b in range(BANDS):
        top[p, b * HALF:(b + 1) * HALF, :] = tile[b, 0:HALF, :]
        bottom[p, b * HALF:(b + 1) * HALF, :] = tile[b, ROWS - HALF:ROWS, :]


def edge_kernel(signs, scale, top, bottom):
    for p in range(signs.shape[0]):
        store_edges(scale[...] * signed(signs[p]), top, bottom, p)


def edges(signs, scale, chunk, count):
    per = 2
    shape = jax.ShapeDtypeStruct((count, BANDS * HALF, COLS), F32)
    return pl.pallas_call(
        edge_kernel, grid=(count // per,), out_shape=(shape, shape),
        in_specs=[
            pl.BlockSpec((per, BANDS, ROWS, COLS), lambda i: (chunk * (count // per) + i, 0, 0, 0)),
            pl.BlockSpec((BANDS, ROWS, COLS), lambda i: (0, 0, 0)),
        ],
        out_specs=[pl.BlockSpec((per, BANDS * HALF, COLS), lambda i: (i, 0, 0))] * 2,
        compiler_params=params(), cost_estimate=cost(1e6, count * 2**19), name="edges",
    )(signs, scale)


def store_packed(tile, left, right, p):
    lane = lax.broadcasted_iota(jnp.int32, (ROWS, 128), 1) // 16
    low = tile[0, :, :128]
    high = pltpu.roll(tile[0, :, 128:], 16, 1)
    for b in range(1, BANDS):
        low = jnp.where(lane == b, pltpu.roll(tile[b, :, :128], 16 * b, 1), low)
        mine = tile[b, :, 128:]
        if b < BANDS - 1:
            mine = pltpu.roll(mine, 16 * b + 16, 1)
        high = jnp.where(lane == b, mine, high)
    left[p] = low
    right[p] = high


def halo_rows(top, bottom, p):
    return jnp.concatenate([top[p], bottom[p], jnp.zeros((16, COLS), F32)], axis=0)


def first_kernel(signs, scale, top, bottom, matrix, out, left, right):
    scaled = (scale[...] * signed(signs[0])).reshape(256, COLS)
    whole = jnp.concatenate([stacked(scaled), stacked(halo_rows(top, bottom, 0))], axis=0)
    tile = dot(matrix[...], whole).reshape(BANDS, ROWS, COLS)
    out[0] = tile
    store_packed(tile, left, right, 0)


def first_stage(signs, scale, top, bottom, matrix, chunk, count):
    packed = jax.ShapeDtypeStruct((count, ROWS, 128), F32)
    tile = pl.BlockSpec((1, BANDS, ROWS, COLS), lambda i: (i, 0, 0, 0))
    edge = pl.BlockSpec((1, BANDS * HALF, COLS), lambda i: (i, 0, 0))
    pack = pl.BlockSpec((1, ROWS, 128), lambda i: (i, 0, 0))
    return pl.pallas_call(
        first_kernel, grid=(count,),
        out_shape=(jax.ShapeDtypeStruct((count, BANDS, ROWS, COLS), F32), packed, packed),
        in_specs=[
            pl.BlockSpec((1, BANDS, ROWS, COLS), lambda i: (chunk * count + i, 0, 0, 0)),
            pl.BlockSpec((BANDS, ROWS, COLS), lambda i: (0, 0, 0)),
            edge, edge,
            pl.BlockSpec((256, 1536), lambda i: (0, 0)),
        ],
        out_specs=[tile, pack, pack],
        compiler_params=params(), cost_estimate=cost(count * 2 * 256 * 1536 * 256, count * 2**20),
        name="first_stage",
    )(signs, scale, top, bottom, matrix)


def column_blur(tiles, left, right, main_h, main_l, halo_h, halo_l, out):
    count = tiles.shape[0]
    flat = count * ROWS
    eh, el = split(jnp.concatenate([left[...], right[...]], axis=-1).reshape(flat, 256))

    @pl.loop(0, BANDS)
    def _(b):
        uh, ul = split(tiles[:, b].reshape(flat, COLS))
        blurred = dot(uh, main_h[b]) + dot(ul, main_h[b]) + dot(uh, main_l[b])
        blurred += dot(eh, halo_h[b]) + dot(el, halo_h[b]) + dot(eh, halo_l[b])
        out[:, b] = blurred.reshape(count, ROWS, COLS)


def middle_kernel(tiles, left, right, main_h, main_l, halo_h, halo_l, mix, back, weights, out, out_left, out_right, blurred):
    column_blur(tiles, left, right, main_h, main_l, halo_h, halo_l, blurred)
    weight = weights[...].reshape(256, COLS)

    @pl.loop(0, tiles.shape[0])
    def _(p):
        weighted = weight * dot(mix[...], stacked(blurred[p].reshape(256, COLS)))
        tile = dot(back[...], stacked(weighted)).reshape(BANDS, ROWS, COLS)
        out[p] = tile
        store_packed(tile, out_left, out_right, p)


def middle_stage(tiles, left, right, tables, mix, back, weights):
    count = tiles.shape[0]
    whole = jax.ShapeDtypeStruct((count, BANDS, ROWS, COLS), F32)
    packed = jax.ShapeDtypeStruct((count, ROWS, 128), F32)
    return pl.pallas_call(
        middle_kernel, out_shape=(whole, packed, packed),
        in_specs=[VMEM] * 10, out_specs=(VMEM,) * 3,
        scratch_shapes=[pltpu.VMEM((count, BANDS, ROWS, COLS), F32)],
        compiler_params=params(), cost_estimate=cost(count * 12 * 2 * 256**3, count * 2**20),
        name="middle_stage",
    )(tiles, left, right, *tables, mix, back, weights)


def last_column_kernel(tiles, left, right, main_h, main_l, halo_h, halo_l, out, top, bottom):
    column_blur(tiles, left, right, main_h, main_l, halo_h, halo_l, out)

    @pl.loop(0, tiles.shape[0])
    def _(p):
        store_edges(out[p], top, bottom, p)


def last_column_stage(tiles, left, right, tables):
    count = tiles.shape[0]
    whole = jax.ShapeDtypeStruct((count, BANDS, ROWS, COLS), F32)
    edge = jax.ShapeDtypeStruct((count, BANDS * HALF, COLS), F32)
    return pl.pallas_call(
        last_column_kernel, out_shape=(whole, edge, edge),
        in_specs=[VMEM] * 7, out_specs=(VMEM,) * 3,
        compiler_params=params(), cost_estimate=cost(count * 6 * 2 * 256**3, count * 2**20),
        name="last_column_stage",
    )(tiles, left, right, *tables)


def sketch_kernel(tiles, top, bottom, matrix, signs, scale, out):
    whole = jnp.concatenate([stacked(tiles[0].reshape(256, COLS)), stacked(halo_rows(top, bottom, 0))], axis=0)
    mixed = dot(matrix[...], whole).reshape(BANDS, ROWS, COLS)
    out[0] = scale[...] * mixed + signed(signs[0])


def sketch_stage(tiles, top, bottom, matrix, signs, scale, chunk):
    count = tiles.shape[0]
    tile = pl.BlockSpec((1, BANDS, ROWS, COLS), lambda i: (i, 0, 0, 0))
    edge = pl.BlockSpec((1, BANDS * HALF, COLS), lambda i: (i, 0, 0))
    return pl.pallas_call(
        sketch_kernel, grid=(count,),
        out_shape=jax.ShapeDtypeStruct((count, BANDS, ROWS, COLS), F32),
        in_specs=[
            tile, edge, edge,
            pl.BlockSpec((256, 1536), lambda i: (0, 0)),
            pl.BlockSpec((1, BANDS, ROWS, COLS), lambda i: (chunk * count + i, 0, 0, 0)),
            pl.BlockSpec((BANDS, ROWS, COLS), lambda i: (0, 0, 0)),
        ],
        out_specs=tile,
        compiler_params=params(), cost_estimate=cost(count * 2 * 256 * 1536 * 256, count * 2**20),
        name="sketch_stage",
    )(tiles, top, bottom, matrix, signs, scale)


def gather_group(refs, g):
    return jnp.concatenate([r[:, g].reshape(-1, COLS) for r in refs], axis=0)


def same_place(shape):
    return lax.broadcasted_iota(jnp.int32, shape, 0) % 8 == lax.broadcasted_iota(jnp.int32, shape, 1) % 8


def spread_ones(shape, long_dim):
    long = lax.broadcasted_iota(jnp.int32, shape, long_dim) // 8
    short = lax.broadcasted_iota(jnp.int32, shape, 1 - long_dim)
    return (long == short).astype(F32)


def gram_kernel(*refs):
    chunks, out, even, cross = refs[:CHUNKS], refs[CHUNKS], refs[CHUNKS + 1], refs[CHUNKS + 2]
    even[...] = jnp.zeros_like(even)
    cross[...] = jnp.zeros_like(cross)

    @pl.loop(0, chunks[0].shape[1])
    def _(g):
        values = gather_group(chunks, g)
        high, middle = split(values)
        low = (values - high.astype(F32) - middle.astype(F32)).astype(BF16)
        even[...] += dot_nt(high, high) + dot_nt(middle, middle)
        cross[...] += dot_nt(high, middle) + dot_nt(high, low)

    order = even.shape[0]
    keep = same_place((order, order))

    def collapse(table):
        kept = jnp.where(keep, table, 0.0)
        return dot(dot(spread_ones((order // 8, order), 1), kept, HI), spread_ones((order, order // 8), 0), HI)

    mixed = collapse(cross[...])
    out[0] = collapse(even[...]) + (mixed + mixed.T)
    out[1] = jnp.zeros(out.shape[1:], F32)


def gram_stage(chunks):
    probes = sum(c.shape[0] for c in chunks)
    return pl.pallas_call(
        gram_kernel, out_shape=jax.ShapeDtypeStruct((2, probes, probes), F32),
        in_specs=[VMEM] * CHUNKS, out_specs=VMEM,
        scratch_shapes=[pltpu.VMEM((256, 256), F32)] * 2,
        compiler_params=params(), cost_estimate=cost(32 * 4 * 2 * 256**3, 2**23), name="gram_stage",
    )(*chunks)


def two_sum(a, b):
    total = a + b
    part = total - a
    return total, (a - (total - part)) + (b - part)


def quick_sum(a, b):
    total = a + b
    return total, b - (total - a)


def halves(a):
    wide = a * 4097.0
    high = wide - (wide - a)
    return high, a - high


def two_product(a, b):
    product = a * b
    ah, al = halves(a)
    bh, bl = halves(b)
    return product, ((ah * bh - product) + ah * bl + al * bh) + al * bl


def pair_add(a, b):
    total, error = two_sum(a[0], b[0])
    return quick_sum(total, error + (a[1] + b[1]))


def pair_mul(a, b):
    product, error = two_product(a[0], b[0])
    return quick_sum(product, error + (a[0] * b[1] + a[1] * b[0]))


def pair_neg(a):
    return -a[0], -a[1]


def merge_kernel(mine, other, out):
    total = pair_add((mine[0], mine[1]), (other[0], other[1]))
    out[0] = total[0]
    out[1] = total[1]


def merge(mine, other):
    return pl.pallas_call(
        merge_kernel, out_shape=jax.ShapeDtypeStruct(mine.shape, F32),
        in_specs=[VMEM] * 2, out_specs=VMEM, compiler_params=params(8), name="merge",
    )(mine, other)


def sum_over(value, axis):
    count = lax.axis_size(axis)
    bit = 1
    while bit < count:
        value = merge(value, lax.ppermute(value, axis, [(i, i ^ bit) for i in range(count)]))
        bit *= 2
    return value


def factor_kernel(gram, factor, inverse, work, *, norm):
    order = gram.shape[1]
    work[...] = jnp.zeros_like(work)
    row = lax.broadcasted_iota(jnp.int32, (order, 128), 0)
    lane = lax.broadcasted_iota(jnp.int32, (order, 128), 1)
    work[0] = (lane == row + order).astype(F32)
    work[0, :, 0:order] = gram[0]
    work[1, :, 0:order] = gram[1]
    now = (work[0], work[1])
    for k in range(order - 1):
        pivot_row = tuple(v[k:k + 1, :] for v in now)
        pivot = tuple(jnp.broadcast_to(v[:, k:k + 1], (1, 128)) for v in pivot_row)
        first = pivot_row[0] / pivot[0]
        rest = pair_add(pivot_row, pair_neg(pair_mul((first, jnp.zeros_like(first)), pivot)))
        ratio = quick_sum(first, rest[0] / pivot[0])
        column = tuple(
            jnp.where(row > k, jnp.broadcast_to(v[:, k:k + 1], (order, 128)), 0.0) for v in now
        )
        now = pair_add(now, pair_neg(pair_mul(column, ratio)))
    diagonal = jnp.sum(jnp.where(lane == row, now[0], 0.0), axis=1, keepdims=True)
    scaled = now[0] / jnp.sqrt(diagonal)
    factor[...] = jnp.where(lane >= row, scaled, 0.0)[:, 0:order] * (1.0 / norm)
    inverse[...] = scaled[:, order:2 * order] * norm


def factor_stage(gram, norm):
    order = gram.shape[1]
    square = jax.ShapeDtypeStruct((order, order), F32)
    return pl.pallas_call(
        lambda *refs: factor_kernel(*refs, norm=norm), out_shape=(square, square),
        in_specs=[VMEM], out_specs=(VMEM, VMEM), scratch_shapes=[pltpu.VMEM((2, order, 128), F32)],
        compiler_params=params(8), name="factor_stage",
    )(gram)


def basis_kernel(inverse, *refs):
    chunks, out, matrix = refs[:CHUNKS], refs[CHUNKS], refs[CHUNKS + 1]
    order = matrix.shape[0]

    @pl.when(pl.program_id(0) == 0)
    def _():
        wide = dot(dot(spread_ones((order, order // 8), 0), inverse[...], HI), spread_ones((order // 8, order), 1), HI)
        high, low = split(jnp.where(same_place((order, order)), wide, 0.0))
        matrix[:, 0:order] = high
        matrix[:, order:2 * order] = low
        matrix[:, 2 * order:3 * order] = high

    @pl.loop(0, chunks[0].shape[1])
    def _(g):
        values = dot(matrix[...], stacked(gather_group(chunks, g)))
        out[:, g] = values.reshape(-1, 8, COLS)


def basis_stage(inverse, chunks):
    probes = inverse.shape[0]
    groups = chunks[0].shape[1]
    per = 4
    return pl.pallas_call(
        basis_kernel, grid=(groups // per,),
        out_shape=jax.ShapeDtypeStruct((probes, groups, 8, COLS), F32),
        in_specs=[pl.BlockSpec((probes, probes), lambda i: (0, 0))]
        + [pl.BlockSpec((c.shape[0], per, 8, COLS), lambda i: (0, i, 0, 0)) for c in chunks],
        out_specs=pl.BlockSpec((probes, per, 8, COLS), lambda i: (0, i, 0, 0)),
        scratch_shapes=[pltpu.VMEM((256, 768), BF16)],
        compiler_params=params(), cost_estimate=cost(32 * 3 * 2 * 256**3, 2**24), name="basis_stage",
    )(inverse, *chunks)


def both_ways(to_previous, to_next, axis):
    count = lax.axis_size(axis)
    forward = [(i, i + 1) for i in range(count - 1)]
    backward = [(i + 1, i) for i in range(count - 1)]
    return lax.ppermute(to_next, axis, forward), lax.ppermute(to_previous, axis, backward)


def shards(probe_signs, prior_scale, prior_factor, band_mix, inverse_noise_variance):
    probes = probe_signs.shape[0]
    count = probes // CHUNKS
    tables = [jnp.asarray(v) for v in col_constants()]
    rows = []
    for k in range(CHUNKS):
        rows.append(both_ways(*edges(probe_signs, prior_scale, k, count), "row"))
    first_m, last_m, mix_m, back_m = prepare(prior_factor, band_mix)
    sketch = []
    for k in range(CHUNKS):
        tiles, left, right = first_stage(probe_signs, prior_scale, *rows[k], first_m, k, count)
        left, right = both_ways(left, right, "col")
        tiles, left, right = middle_stage(tiles, left, right, tables, mix_m, back_m, inverse_noise_variance)
        left, right = both_ways(left, right, "col")
        tiles, top, bottom = last_column_stage(tiles, left, right, tables)
        top, bottom = both_ways(top, bottom, "row")
        sketch.append(sketch_stage(tiles, top, bottom, last_m, probe_signs, prior_scale, k))
    grouped = [s.reshape(count, BANDS * ROWS // 8, 8, COLS) for s in sketch]
    gram = sum_over(sum_over(gram_stage(grouped), "row"), "col")
    total = BANDS * ROWS * COLS * lax.axis_size("row") * lax.axis_size("col")
    r_factor, inverse = factor_stage(gram, float(np.sqrt(np.float32(total))))
    basis = basis_stage(inverse, grouped)
    return basis.reshape(probes, BANDS, ROWS, COLS), r_factor


def solution(mesh):
    in_specs = (P(None, None, "row", "col"), P(None, "row", "col"), P(), P(), P(None, "row", "col"))
    out_specs = (P(None, None, "row", "col"), P())
    return jax.shard_map(shards, mesh=mesh, in_specs=in_specs, out_specs=out_specs, check_vma=False)
```

```python
import numpy as np
import jax
import jax.numpy as jnp
from jax import lax
from jax.experimental import pallas as pl
from jax.experimental.pallas import tpu as pltpu
from jax.sharding import PartitionSpec as P

BANDS = 8
HALF = 15
TAPS = 31
ROWS = 32
COLS = 256
CHUNKS = (8, 12, 12)
PER = 4

F32 = jnp.float32
BF16 = jnp.bfloat16
HI = lax.Precision.HIGHEST
VMEM = pl.BlockSpec(memory_space=pltpu.VMEM)
SMEM = pl.BlockSpec(memory_space=pltpu.SMEM)
SIDE = jax.ShapeDtypeStruct((2,), jnp.int32)


def taps_np():
    offsets = np.arange(TAPS) - HALF
    sigma = 1.0 + 0.5 * np.arange(BANDS)
    raw = np.exp(-offsets[None, :] ** 2 / (2.0 * sigma[:, None] ** 2))
    return raw / raw.sum(axis=1, keepdims=True)


def table_np(pos_in, pos_out):
    taps = taps_np()
    offset = np.asarray(pos_in)[:, None] - np.asarray(pos_out)[None, :]
    inside = np.abs(offset) <= HALF
    return np.where(inside[None], taps[:, np.clip(offset + HALF, 0, TAPS - 1)], 0.0)


def split_np(values):
    high = values.astype(BF16)
    low = (values - high.astype(np.float64)).astype(BF16)
    return high, low


def row_constants():
    out = np.arange(ROWS)
    main = table_np(np.arange(ROWS), out)
    above = table_np(np.arange(-HALF, 0), out)
    below = table_np(np.arange(ROWS, ROWS + HALF), out)
    by_out = np.zeros((BANDS, ROWS, 512))
    by_in = np.zeros((BANDS, ROWS, 512))
    pick = np.zeros((BANDS, 512))
    for c in range(BANDS):
        parts = ((c * ROWS, ROWS, main), (256 + c * HALF, HALF, above), (376 + c * HALF, HALF, below))
        for start, size, table in parts:
            by_out[:, :, start:start + size] = table.transpose(0, 2, 1)
            by_in[:, :, start:start + size] = table[c].T[None]
            pick[c, start:start + size] = 1.0
    spread = np.repeat(np.eye(BANDS), ROWS, axis=0)
    same = np.tile(np.eye(ROWS), (BANDS, BANDS))
    return [v.astype(np.float32) for v in (by_out.reshape(256, 512), by_in.reshape(256, 512), pick, spread, same)]


def col_constants():
    out = np.arange(COLS)
    main = table_np(np.arange(COLS), out)
    left = table_np(np.arange(-16, 0), out)
    right = table_np(np.arange(COLS, COLS + 16), out)
    main_h, main_l = split_np(main)
    halo_h, halo_l = split_np(np.concatenate([left, right], axis=1))
    halo = np.zeros((BANDS, 256, COLS), BF16)
    halo[:, 0:32] = halo_h
    halo[:, 32:64] = halo_l
    halo[:, 128:160] = halo_h
    return np.concatenate([main_h, main_h, main_l, halo], axis=1)


def split(values):
    high = values.astype(BF16)
    return high, (values - high.astype(F32)).astype(BF16)


def dot(a, b, precision=None):
    return lax.dot_general(a, b, (((1,), (0,)), ((), ())), precision=precision, preferred_element_type=F32)


def dot_nt(a, b):
    return lax.dot_general(a, b, (((1,), (1,)), ((), ())), preferred_element_type=F32)


def stacked(values):
    high, low = split(values)
    return jnp.concatenate([high, high, low], axis=0)


def hand_on(side, after):
    after[0] = side[0]
    after[1] = side[1]


def params(mib=24):
    return pltpu.CompilerParams(vmem_limit_bytes=mib * 2**20)


def cost(flops, moved):
    return pl.CostEstimate(flops=int(flops), bytes_accessed=int(moved), transcendentals=0)


def prepare_kernel(side, factor, mix, by_out, by_in, pick, spread, same, first_m, last_m, mix_m, back_m):
    lower = side[0] == 0
    def expand(small, right):
        return dot(dot(spread[...], small, HI), right, HI)

    def store(out, whole):
        for part in range(whole.shape[1] // 256):
            high, low = split(whole[:, part * 256:part * 256 + 256])
            out[:, part * 768:part * 768 + 256] = high
            out[:, part * 768 + 256:part * 768 + 512] = low
            out[:, part * 768 + 512:part * 768 + 768] = high

    f = factor[...]
    a = mix[...]

    def ordered(table):
        whole = table[...]
        above, below, rest = whole[:, 256:376], whole[:, 376:496], whole[:, 496:512]
        swapped = jnp.concatenate([whole[:, 0:256], below, above, rest], axis=1)
        return jnp.where(lower, whole, swapped)

    store(first_m, expand(f, pick[...]) * ordered(by_out))
    store(last_m, expand(f.T, pick[...]) * ordered(by_in))
    store(mix_m, expand(a, pick[:, :256]) * same[...])
    store(back_m, expand(a.T, pick[:, :256]) * same[...])


def prepare(side, factor, mix):
    wide = jax.ShapeDtypeStruct((256, 1536), BF16)
    narrow = jax.ShapeDtypeStruct((256, 768), BF16)
    return pl.pallas_call(
        prepare_kernel, out_shape=(wide, wide, narrow, narrow),
        in_specs=[SMEM] + [VMEM] * 7, out_specs=(VMEM,) * 4, compiler_params=params(),
        name="prepare",
    )(side, factor, mix, *[jnp.asarray(v) for v in row_constants()])


def signed(ref_value):
    return 2.0 * ref_value.astype(F32) - 1.0


def store_edges(tile, top, bottom, p):
    for b in range(BANDS):
        top[p, b * HALF:(b + 1) * HALF, :] = tile[b, 0:HALF, :]
        bottom[p, b * HALF:(b + 1) * HALF, :] = tile[b, ROWS - HALF:ROWS, :]


def store_by_side(tile, lower, inner, outer, p):
    @pl.when(lower)
    def _():
        store_edges(tile, outer, inner, p)

    @pl.when(jnp.logical_not(lower))
    def _():
        store_edges(tile, inner, outer, p)


def edge_kernel(side, signs, scale, inner, outer):
    for p in range(signs.shape[0]):
        store_by_side(scale[...] * signed(signs[p]), side[0] == 0, inner, outer, p)


def edges(side, signs, scale):
    count = signs.shape[0]
    shape = jax.ShapeDtypeStruct((count, BANDS * HALF, COLS), F32)
    return pl.pallas_call(
        edge_kernel, grid=(count // PER,), out_shape=(shape, shape),
        in_specs=[
            SMEM,
            pl.BlockSpec((PER, BANDS, ROWS, COLS), lambda i: (i, 0, 0, 0)),
            pl.BlockSpec((BANDS, ROWS, COLS), lambda i: (0, 0, 0)),
        ],
        out_specs=[pl.BlockSpec((PER, BANDS * HALF, COLS), lambda i: (i, 0, 0))] * 2,
        compiler_params=params(), cost_estimate=cost(1e6, count * 2**19), name="edges",
    )(side, signs, scale)


def store_packed(tile, lower, near, far, p):
    lane = lax.broadcasted_iota(jnp.int32, (ROWS, 128), 1) // 16
    low = tile[0, :, :128]
    high = pltpu.roll(tile[0, :, 128:], 16, 1)
    for b in range(1, BANDS):
        low = jnp.where(lane == b, pltpu.roll(tile[b, :, :128], 16 * b, 1), low)
        mine = tile[b, :, 128:]
        if b < BANDS - 1:
            mine = pltpu.roll(mine, 16 * b + 16, 1)
        high = jnp.where(lane == b, mine, high)
    near[p] = jnp.where(lower, high, low)
    far[p] = jnp.where(lower, low, high)


def halo_rows(outer, inner, p):
    return jnp.concatenate([outer[p], inner[p], jnp.zeros((16, COLS), F32)], axis=0)


def first_kernel(side, signs, scale, inner, outer, matrix, out, near, far, after):
    hand_on(side, after)

    @pl.loop(0, out.shape[0], step=PER)
    def _(start):
        for p in range(PER):
            scaled = (scale[...] * signed(signs[start + p])).reshape(256, COLS)
            whole = jnp.concatenate([stacked(scaled), stacked(halo_rows(outer, inner, start + p))], axis=0)
            tile = dot(matrix[...], whole).reshape(BANDS, ROWS, COLS)
            out[start + p] = tile
            store_packed(tile, side[1] == 0, near, far, start + p)


def first_stage(side, signs, scale, inner, outer, matrix):
    count = signs.shape[0]
    packed = jax.ShapeDtypeStruct((count, ROWS, 128), F32)
    return pl.pallas_call(
        first_kernel,
        out_shape=(jax.ShapeDtypeStruct((count, BANDS, ROWS, COLS), F32), packed, packed, SIDE),
        in_specs=[SMEM] + [VMEM] * 5, out_specs=(VMEM, VMEM, VMEM, SMEM),
        compiler_params=params(), cost_estimate=cost(count * 2 * 256 * 1536 * 256, count * 2**20),
        name="first_stage",
    )(side, signs, scale, inner, outer, matrix)


def column_blur(lower, tiles, near, far, table, out):
    count = tiles.shape[0]
    flat = count * ROWS
    first = near[...].reshape(flat, 128)
    other = far[...].reshape(flat, 128)
    left = jnp.where(lower, other, first)
    right = jnp.where(lower, first, other)
    lane = lax.broadcasted_iota(jnp.int32, (flat, 128), 1)

    @pl.loop(0, BANDS, step=4)
    def _(start):
        for b in [start + j for j in range(4)]:
            uh, ul = split(tiles[:, b].reshape(flat, COLS))
            sides = jnp.where(lane < 16, pltpu.roll(left, 128 - 16 * b, 1), pltpu.roll(right, (144 - 16 * b) % 128, 1))
            sides = jnp.where(lane < 32, sides, pltpu.roll(sides, 32, 1))
            eh, el = split(sides)
            blurred = dot(jnp.concatenate([uh, ul, uh, eh, el], axis=1), table[b])
            out[:, b] = blurred.reshape(count, ROWS, COLS)


def middle_kernel(side, tiles, near, far, table, mix, back, weights, out, out_near, out_far, after, blurred):
    hand_on(side, after)
    lower = side[1] == 0
    column_blur(lower, tiles, near, far, table, blurred)
    weight = weights[...].reshape(256, COLS)

    group = 6 if tiles.shape[0] % 6 == 0 else 8

    @pl.loop(0, tiles.shape[0], step=group)
    def _(start):
        for p in range(group):
            weighted = weight * dot(mix[...], stacked(blurred[start + p].reshape(256, COLS)))
            tile = dot(back[...], stacked(weighted)).reshape(BANDS, ROWS, COLS)
            out[start + p] = tile
            store_packed(tile, lower, out_near, out_far, start + p)


def middle_stage(side, tiles, near, far, table, mix, back, weights):
    count = tiles.shape[0]
    whole = jax.ShapeDtypeStruct((count, BANDS, ROWS, COLS), F32)
    packed = jax.ShapeDtypeStruct((count, ROWS, 128), F32)
    return pl.pallas_call(
        middle_kernel, out_shape=(whole, packed, packed, SIDE),
        in_specs=[SMEM] + [VMEM] * 7, out_specs=(VMEM, VMEM, VMEM, SMEM),
        scratch_shapes=[pltpu.VMEM((count, BANDS, ROWS, COLS), F32)],
        compiler_params=params(), cost_estimate=cost(count * 10 * 2 * 256**3, count * 2**20),
        name="middle_stage",
    )(side, tiles, near, far, table, mix, back, weights)


def last_column_kernel(side, tiles, near, far, table, out, inner, outer, after):
    hand_on(side, after)
    column_blur(side[1] == 0, tiles, near, far, table, out)

    @pl.when(side[0] == 0)
    def _():
        @pl.loop(0, tiles.shape[0], step=PER)
        def _(start):
            for p in range(PER):
                store_edges(out[start + p], outer, inner, start + p)

    @pl.when(side[0] != 0)
    def _():
        @pl.loop(0, tiles.shape[0], step=PER)
        def _(start):
            for p in range(PER):
                store_edges(out[start + p], inner, outer, start + p)


def last_column_stage(side, tiles, near, far, table):
    count = tiles.shape[0]
    whole = jax.ShapeDtypeStruct((count, BANDS, ROWS, COLS), F32)
    edge = jax.ShapeDtypeStruct((count, BANDS * HALF, COLS), F32)
    return pl.pallas_call(
        last_column_kernel, out_shape=(whole, edge, edge, SIDE),
        in_specs=[SMEM] + [VMEM] * 4, out_specs=(VMEM, VMEM, VMEM, SMEM),
        compiler_params=params(), cost_estimate=cost(count * 4 * 2 * 256**3, count * 2**20),
        name="last_column_stage",
    )(side, tiles, near, far, table)


def sketch_kernel(side, tiles, inner, outer, matrix, signs, scale, out, after):
    hand_on(side, after)

    @pl.loop(0, out.shape[0], step=PER)
    def _(start):
        for p in range(PER):
            spot = start + p
            whole = jnp.concatenate(
                [stacked(tiles[spot].reshape(256, COLS)), stacked(halo_rows(outer, inner, spot))], axis=0
            )
            mixed = dot(matrix[...], whole).reshape(BANDS, ROWS, COLS)
            out[spot] = scale[...] * mixed + signed(signs[spot])


def sketch_stage(side, tiles, inner, outer, matrix, signs, scale):
    count = tiles.shape[0]
    return pl.pallas_call(
        sketch_kernel, out_shape=(jax.ShapeDtypeStruct((count, BANDS, ROWS, COLS), F32), SIDE),
        in_specs=[SMEM] + [VMEM] * 6, out_specs=(VMEM, SMEM),
        compiler_params=params(), cost_estimate=cost(count * 2 * 256 * 1536 * 256, count * 2**20),
        name="sketch_stage",
    )(side, tiles, inner, outer, matrix, signs, scale)


def gather_group(refs, g):
    return jnp.concatenate([r[:, g].reshape(-1, COLS) for r in refs], axis=0)


def same_place(shape):
    return lax.broadcasted_iota(jnp.int32, shape, 0) % 8 == lax.broadcasted_iota(jnp.int32, shape, 1) % 8


def spread_ones(shape, long_dim):
    long = lax.broadcasted_iota(jnp.int32, shape, long_dim) // 8
    short = lax.broadcasted_iota(jnp.int32, shape, 1 - long_dim)
    return (long == short).astype(F32)


def gram_kernel(*refs):
    chunks, out, even, cross = refs[:-3], refs[-3], refs[-2], refs[-1]
    even[...] = jnp.zeros_like(even)
    cross[...] = jnp.zeros_like(cross)

    @pl.loop(0, chunks[0].shape[1], step=8)
    def _(g):
        values = jnp.concatenate([gather_group(chunks, g + j) for j in range(8)], axis=1)
        high, low = split(values)
        even[...] += dot_nt(high, high) + dot_nt(low, low)
        cross[...] += dot_nt(high, low)

    order = even.shape[0]
    keep = same_place((order, order))

    def collapse(table):
        kept = jnp.where(keep, table, 0.0)
        return dot(dot(spread_ones((order // 8, order), 1), kept, HI), spread_ones((order, order // 8), 0), HI)

    mixed = collapse(cross[...])
    total = collapse(even[...]) + (mixed + mixed.T)
    out[0] = jnp.concatenate([total[8 * j:8 * j + 8] for j in range(4)], axis=1)
    out[1] = jnp.zeros(out.shape[1:], F32)


def gram_stage(chunks):
    probes = sum(c.shape[0] for c in chunks)
    return pl.pallas_call(
        gram_kernel, out_shape=jax.ShapeDtypeStruct((2, 8, 128), F32),
        in_specs=[VMEM] * len(chunks), out_specs=VMEM,
        scratch_shapes=[pltpu.VMEM((256, 256), F32)] * 2,
        compiler_params=params(), cost_estimate=cost(32 * 4 * 2 * 256**3, 2**23), name="gram_stage",
    )(*chunks)


def group_blocks(chunks):
    return [pl.BlockSpec((c.shape[0], PER, 8, COLS), lambda i: (0, i, 0, 0)) for c in chunks]


def two_sum(a, b):
    total = a + b
    part = total - a
    return total, (a - (total - part)) + (b - part)


def quick_sum(a, b):
    total = a + b
    return total, b - (total - a)


def halves(a):
    wide = a * 4097.0
    high = wide - (wide - a)
    return high, a - high


def two_product(a, b):
    product = a * b
    ah, al = halves(a)
    bh, bl = halves(b)
    return product, ((ah * bh - product) + ah * bl + al * bh) + al * bl


def pair_add(a, b):
    total, error = two_sum(a[0], b[0])
    return quick_sum(total, error + (a[1] + b[1]))


def pair_mul(a, b):
    product, error = two_product(a[0], b[0])
    return quick_sum(product, error + (a[0] * b[1] + a[1] * b[0]))


def pair_neg(a):
    return -a[0], -a[1]


def merge_kernel(mine, other, out):
    total = pair_add((mine[0], mine[1]), (other[0], other[1]))
    out[0] = total[0]
    out[1] = total[1]


def merge(mine, other):
    return pl.pallas_call(
        merge_kernel, out_shape=jax.ShapeDtypeStruct(mine.shape, F32),
        in_specs=[VMEM] * 2, out_specs=VMEM, compiler_params=params(), name="merge",
    )(mine, other)


def sum_over(value, axis):
    count = lax.axis_size(axis)
    bit = 1
    while bit < count:
        value = merge(value, lax.ppermute(value, axis, [(i, i ^ bit) for i in range(count)]))
        bit *= 2
    return value


def factor_kernel(gram, factor, inverse, work, *, norm):
    order = factor.shape[0]
    work[...] = jnp.zeros_like(work)
    row = lax.broadcasted_iota(jnp.int32, (order, 128), 0)
    lane = lax.broadcasted_iota(jnp.int32, (order, 128), 1)
    work[0] = (lane == row + order).astype(F32)
    for j in range(4):
        work[:, 8 * j:8 * j + 8, 0:order] = gram[:, :, j * order:(j + 1) * order]
    now = (work[0], work[1])
    for k in range(order - 1):
        pivot_row = tuple(v[k:k + 1, :] for v in now)
        pivot = tuple(jnp.broadcast_to(v[:, k:k + 1], (1, 128)) for v in pivot_row)
        first = pivot_row[0] / pivot[0]
        rest = pair_add(pivot_row, pair_neg(pair_mul((first, jnp.zeros_like(first)), pivot)))
        ratio = quick_sum(first, rest[0] / pivot[0])
        column = tuple(
            jnp.where(row > k, jnp.broadcast_to(v[:, k:k + 1], (order, 128)), 0.0) for v in now
        )
        now = pair_add(now, pair_neg(pair_mul(column, ratio)))
    diagonal = jnp.sum(jnp.where(lane == row, now[0], 0.0), axis=1, keepdims=True)
    scaled = now[0] / jnp.sqrt(diagonal)
    factor[...] = jnp.where(lane >= row, scaled, 0.0)[:, 0:order] * (1.0 / norm)
    inverse[...] = scaled[:, order:2 * order] * norm


def factor_stage(gram, order, norm):
    square = jax.ShapeDtypeStruct((order, order), F32)
    return pl.pallas_call(
        lambda *refs: factor_kernel(*refs, norm=norm), out_shape=(square, square),
        in_specs=[VMEM], out_specs=(VMEM, VMEM), scratch_shapes=[pltpu.VMEM((2, order, 128), F32)],
        compiler_params=params(), name="factor_stage",
    )(gram)


def basis_kernel(inverse, *refs):
    chunks, out, matrix = refs[:-2], refs[-2], refs[-1]
    order = matrix.shape[0]

    @pl.when(pl.program_id(0) == 0)
    def _():
        wide = dot(dot(spread_ones((order, order // 8), 0), inverse[...], HI), spread_ones((order // 8, order), 1), HI)
        high, low = split(jnp.where(same_place((order, order)), wide, 0.0))
        matrix[:, 0:order] = high
        matrix[:, order:2 * order] = low
        matrix[:, 2 * order:3 * order] = high

    start = pl.program_id(0) * out.shape[1]
    for g in range(out.shape[1]):
        values = dot(matrix[...], stacked(gather_group(chunks, start + g)))
        out[:, g] = values.reshape(-1, 8, COLS)


def basis_stage(inverse, chunks):
    probes = inverse.shape[0]
    groups = chunks[0].shape[1]
    return pl.pallas_call(
        basis_kernel, grid=(groups // 8,),
        out_shape=jax.ShapeDtypeStruct((probes, groups, 8, COLS), F32),
        in_specs=[VMEM] * (1 + len(chunks)),
        out_specs=pl.BlockSpec((probes, 8, 8, COLS), lambda i: (0, i, 0, 0)),
        scratch_shapes=[pltpu.VMEM((256, 768), BF16)],
        compiler_params=params(), cost_estimate=cost(32 * 3 * 2 * 256**3, 2**24), name="basis_stage",
    )(inverse, *chunks)


def swap(inner, outer, axis):
    count = lax.axis_size(axis)
    pairs = [(i, i ^ 1) for i in range(count)]
    others = [p for i in range(1, count - 1, 2) for p in ((i, i + 1), (i + 1, i))]
    return lax.ppermute(inner, axis, pairs), lax.ppermute(outer, axis, others)


def shards(probe_signs, prior_scale, prior_factor, band_mix, inverse_noise_variance):
    probes = probe_signs.shape[0]
    side = jnp.stack([lax.axis_index("row") % 2, lax.axis_index("col") % 2]).astype(jnp.int32)
    table = jnp.asarray(col_constants())
    starts = [sum(CHUNKS[:k]) for k in range(len(CHUNKS))]
    signs = [probe_signs[start:start + count] for start, count in zip(starts, CHUNKS)]
    rows = [swap(*edges(side, part, prior_scale), "row") for part in signs]
    first_m, last_m, mix_m, back_m = prepare(side, prior_factor, band_mix)
    last = len(CHUNKS) - 1
    state = {}

    def first(k, side):
        *state[k], side = first_stage(side, signs[k], prior_scale, *rows[k], first_m)
        state[k][1:] = swap(*state[k][1:], "col")
        return side

    def middle(k, side):
        *state[k], side = middle_stage(side, *state[k], table, mix_m, back_m, inverse_noise_variance)
        state[k][1:] = swap(*state[k][1:], "col")
        return side

    def last_column(k, side):
        *state[k], side = last_column_stage(side, *state[k], table)
        state[k][1:] = swap(*state[k][1:], "row")
        return side

    def finish(k, side):
        state[k], side = sketch_stage(side, *state[k], last_m, signs[k], prior_scale)
        return side

    side = first(0, side)
    side = middle(0, side)
    for k in range(1, last + 1):
        side = first(k, side)
        side = last_column(k - 1, side)
        side = middle(k, side)
    for k in range(last - 1):
        side = finish(k, side)
    side = last_column(last, side)
    for k in range(max(last - 1, 0), last + 1):
        side = finish(k, side)
    sketch = [state[k] for k in range(last + 1)]
    grouped = [s.reshape(s.shape[0], BANDS * ROWS // 8, 8, COLS) for s in sketch]
    gram = sum_over(sum_over(gram_stage(grouped), "row"), "col")
    total = BANDS * ROWS * COLS * lax.axis_size("row") * lax.axis_size("col")
    r_factor, inverse = factor_stage(gram, probes, float(np.sqrt(np.float32(total))))
    basis = basis_stage(inverse, grouped)
    return basis.reshape(probes, BANDS, ROWS, COLS), r_factor


def solution(mesh):
    in_specs = (P(None, None, "row", "col"), P(None, "row", "col"), P(), P(), P(None, "row", "col"))
    out_specs = (P(None, None, "row", "col"), P())
    return jax.shard_map(shards, mesh=mesh, in_specs=in_specs, out_specs=out_specs, check_vma=False)
```

```python
import numpy as np
import jax
import jax.numpy as jnp
from jax import lax
from jax.experimental import pallas as pl
from jax.experimental.pallas import tpu as pltpu
from jax.sharding import PartitionSpec as P

BANDS = 8
HALF = 15
TAPS = 31
ROWS = 32
COLS = 256
CHUNKS = (8, 12, 12)
PER = 4

F32 = jnp.float32
BF16 = jnp.bfloat16
HI = lax.Precision.HIGHEST
VMEM = pl.BlockSpec(memory_space=pltpu.VMEM)
SMEM = pl.BlockSpec(memory_space=pltpu.SMEM)
SIDE = jax.ShapeDtypeStruct((2,), jnp.int32)


def taps_np():
    offsets = np.arange(TAPS) - HALF
    sigma = 1.0 + 0.5 * np.arange(BANDS)
    raw = np.exp(-offsets[None, :] ** 2 / (2.0 * sigma[:, None] ** 2))
    return raw / raw.sum(axis=1, keepdims=True)


def table_np(pos_in, pos_out):
    taps = taps_np()
    offset = np.asarray(pos_in)[:, None] - np.asarray(pos_out)[None, :]
    inside = np.abs(offset) <= HALF
    return np.where(inside[None], taps[:, np.clip(offset + HALF, 0, TAPS - 1)], 0.0)


def split_np(values):
    high = values.astype(BF16)
    low = (values - high.astype(np.float64)).astype(BF16)
    return high, low


def row_constants():
    out = np.arange(ROWS)
    main = table_np(np.arange(ROWS), out)
    above = table_np(np.arange(-HALF, 0), out)
    below = table_np(np.arange(ROWS, ROWS + HALF), out)
    by_out = np.zeros((BANDS, ROWS, 512))
    by_in = np.zeros((BANDS, ROWS, 512))
    pick = np.zeros((BANDS, 512))
    for c in range(BANDS):
        parts = ((c * ROWS, ROWS, main), (256 + c * HALF, HALF, above), (376 + c * HALF, HALF, below))
        for start, size, table in parts:
            by_out[:, :, start:start + size] = table.transpose(0, 2, 1)
            by_in[:, :, start:start + size] = table[c].T[None]
            pick[c, start:start + size] = 1.0
    spread = np.repeat(np.eye(BANDS), ROWS, axis=0)
    same = np.tile(np.eye(ROWS), (BANDS, BANDS))
    return [v.astype(np.float32) for v in (by_out.reshape(256, 512), by_in.reshape(256, 512), pick, spread, same)]


def col_constants():
    out = np.arange(COLS)
    main = table_np(np.arange(COLS), out)
    left = table_np(np.arange(-16, 0), out)
    right = table_np(np.arange(COLS, COLS + 16), out)
    main_h, main_l = split_np(main)
    halo_h, halo_l = split_np(np.concatenate([left, right], axis=1))
    halo = np.zeros((BANDS, 256, COLS), BF16)
    halo[:, 0:32] = halo_h
    halo[:, 32:64] = halo_l
    halo[:, 128:160] = halo_h
    return np.concatenate([main_h, main_h, main_l, halo], axis=1)


def split(values):
    high = values.astype(BF16)
    return high, (values - high.astype(F32)).astype(BF16)


def dot(a, b, precision=None):
    return lax.dot_general(a, b, (((1,), (0,)), ((), ())), precision=precision, preferred_element_type=F32)


def dot_nt(a, b):
    return lax.dot_general(a, b, (((1,), (1,)), ((), ())), preferred_element_type=F32)


def stacked(values):
    high, low = split(values)
    return jnp.concatenate([high, high, low], axis=0)


def hand_on(side, after):
    after[0] = side[0]
    after[1] = side[1]


def params(mib=24):
    return pltpu.CompilerParams(vmem_limit_bytes=mib * 2**20)


def cost(flops, moved):
    return pl.CostEstimate(flops=int(flops), bytes_accessed=int(moved), transcendentals=0)


def prepare_kernel(side, factor, mix, by_out, by_in, pick, spread, same, first_m, last_m, mix_m, back_m):
    lower = side[0] == 0
    def expand(small, right):
        return dot(dot(spread[...], small, HI), right, HI)

    def store(out, whole):
        for part in range(whole.shape[1] // 256):
            high, low = split(whole[:, part * 256:part * 256 + 256])
            out[:, part * 768:part * 768 + 256] = high
            out[:, part * 768 + 256:part * 768 + 512] = low
            out[:, part * 768 + 512:part * 768 + 768] = high

    f = factor[...]
    a = mix[...]

    def ordered(table):
        whole = table[...]
        above, below, rest = whole[:, 256:376], whole[:, 376:496], whole[:, 496:512]
        swapped = jnp.concatenate([whole[:, 0:256], below, above, rest], axis=1)
        return jnp.where(lower, whole, swapped)

    store(first_m, expand(f, pick[...]) * ordered(by_out))
    store(last_m, expand(f.T, pick[...]) * ordered(by_in))
    store(mix_m, expand(a, pick[:, :256]) * same[...])
    store(back_m, expand(a.T, pick[:, :256]) * same[...])


def prepare(side, factor, mix):
    wide = jax.ShapeDtypeStruct((256, 1536), BF16)
    narrow = jax.ShapeDtypeStruct((256, 768), BF16)
    return pl.pallas_call(
        prepare_kernel, out_shape=(wide, wide, narrow, narrow),
        in_specs=[SMEM] + [VMEM] * 7, out_specs=(VMEM,) * 4, compiler_params=params(),
        name="prepare",
    )(side, factor, mix, *[jnp.asarray(v) for v in row_constants()])


def signed(ref_value):
    return 2.0 * ref_value.astype(F32) - 1.0


def store_edges(tile, top, bottom, p):
    for b in range(BANDS):
        top[p, b * HALF:(b + 1) * HALF, :] = tile[b, 0:HALF, :]
        bottom[p, b * HALF:(b + 1) * HALF, :] = tile[b, ROWS - HALF:ROWS, :]


def store_by_side(tile, lower, inner, outer, p):
    @pl.when(lower)
    def _():
        store_edges(tile, outer, inner, p)

    @pl.when(jnp.logical_not(lower))
    def _():
        store_edges(tile, inner, outer, p)


def edge_kernel(side, signs, scale, inner, outer):
    for p in range(signs.shape[0]):
        store_by_side(scale[...] * signed(signs[p]), side[0] == 0, inner, outer, p)


def edges(side, signs, scale):
    count = signs.shape[0]
    shape = jax.ShapeDtypeStruct((count, BANDS * HALF, COLS), F32)
    return pl.pallas_call(
        edge_kernel, grid=(count // PER,), out_shape=(shape, shape),
        in_specs=[
            SMEM,
            pl.BlockSpec((PER, BANDS, ROWS, COLS), lambda i: (i, 0, 0, 0)),
            pl.BlockSpec((BANDS, ROWS, COLS), lambda i: (0, 0, 0)),
        ],
        out_specs=[pl.BlockSpec((PER, BANDS * HALF, COLS), lambda i: (i, 0, 0))] * 2,
        compiler_params=params(), cost_estimate=cost(1e6, count * 2**19), name="edges",
    )(side, signs, scale)


def store_packed(tile, lower, near, far, p):
    lane = lax.broadcasted_iota(jnp.int32, (ROWS, 128), 1) // 16
    low = tile[0, :, :128]
    high = pltpu.roll(tile[0, :, 128:], 16, 1)
    for b in range(1, BANDS):
        low = jnp.where(lane == b, pltpu.roll(tile[b, :, :128], 16 * b, 1), low)
        mine = tile[b, :, 128:]
        if b < BANDS - 1:
            mine = pltpu.roll(mine, 16 * b + 16, 1)
        high = jnp.where(lane == b, mine, high)
    near[p] = jnp.where(lower, high, low)
    far[p] = jnp.where(lower, low, high)


def halo_rows(outer, inner, p):
    return jnp.concatenate([outer[p], inner[p], jnp.zeros((16, COLS), F32)], axis=0)


def first_kernel(side, signs, scale, inner, outer, matrix, out, near, far, after):
    hand_on(side, after)

    @pl.loop(0, out.shape[0], step=PER)
    def _(start):
        for p in range(PER):
            scaled = (scale[...] * signed(signs[start + p])).reshape(256, COLS)
            whole = jnp.concatenate([stacked(scaled), stacked(halo_rows(outer, inner, start + p))], axis=0)
            tile = dot(matrix[...], whole).reshape(BANDS, ROWS, COLS)
            out[start + p] = tile
            store_packed(tile, side[1] == 0, near, far, start + p)


def first_stage(side, signs, scale, inner, outer, matrix):
    count = signs.shape[0]
    packed = jax.ShapeDtypeStruct((count, ROWS, 128), F32)
    return pl.pallas_call(
        first_kernel,
        out_shape=(jax.ShapeDtypeStruct((count, BANDS, ROWS, COLS), F32), packed, packed, SIDE),
        in_specs=[SMEM] + [VMEM] * 5, out_specs=(VMEM, VMEM, VMEM, SMEM),
        compiler_params=params(), cost_estimate=cost(count * 2 * 256 * 1536 * 256, count * 2**20),
        name="first_stage",
    )(side, signs, scale, inner, outer, matrix)


def column_blur(lower, tiles, near, far, table, out):
    count = tiles.shape[0]
    flat = count * ROWS
    first = near[...].reshape(flat, 128)
    other = far[...].reshape(flat, 128)
    left = jnp.where(lower, other, first)
    right = jnp.where(lower, first, other)
    lane = lax.broadcasted_iota(jnp.int32, (flat, 128), 1)

    @pl.loop(0, BANDS, step=4)
    def _(start):
        for b in [start + j for j in range(4)]:
            uh, ul = split(tiles[:, b].reshape(flat, COLS))
            sides = jnp.where(lane < 16, pltpu.roll(left, 128 - 16 * b, 1), pltpu.roll(right, (144 - 16 * b) % 128, 1))
            sides = jnp.where(lane < 32, sides, pltpu.roll(sides, 32, 1))
            eh, el = split(sides)
            blurred = dot(jnp.concatenate([uh, ul, uh, eh, el], axis=1), table[b])
            out[:, b] = blurred.reshape(count, ROWS, COLS)


def middle_kernel(side, tiles, near, far, table, mix, back, weights, ahead, out, out_near, out_far, after, blurred):
    hand_on(side, after)
    lower = side[1] == 0
    column_blur(lower, tiles, near, far, table, blurred)
    weight = weights[...].reshape(256, COLS)

    group = 6 if tiles.shape[0] % 6 == 0 else 8

    @pl.loop(0, tiles.shape[0], step=group)
    def _(start):
        for p in range(group):
            weighted = weight * dot(mix[...], stacked(blurred[start + p].reshape(256, COLS)))
            tile = dot(back[...], stacked(weighted)).reshape(BANDS, ROWS, COLS)
            out[start + p] = tile
            store_packed(tile, lower, out_near, out_far, start + p)


def middle_stage(side, tiles, near, far, table, mix, back, weights, ahead):
    ahead = side if ahead is None else ahead
    count = tiles.shape[0]
    whole = jax.ShapeDtypeStruct((count, BANDS, ROWS, COLS), F32)
    packed = jax.ShapeDtypeStruct((count, ROWS, 128), F32)
    return pl.pallas_call(
        middle_kernel, out_shape=(whole, packed, packed, SIDE),
        in_specs=[SMEM] + [VMEM] * 7 + [pl.BlockSpec(memory_space=pl.ANY)], out_specs=(VMEM, VMEM, VMEM, SMEM),
        scratch_shapes=[pltpu.VMEM((count, BANDS, ROWS, COLS), F32)],
        compiler_params=params(), cost_estimate=cost(count * 10 * 2 * 256**3, count * 2**20),
        name="middle_stage",
    )(side, tiles, near, far, table, mix, back, weights, ahead)


def last_column_kernel(side, tiles, near, far, table, out, inner, outer, after):
    hand_on(side, after)
    column_blur(side[1] == 0, tiles, near, far, table, out)

    @pl.when(side[0] == 0)
    def _():
        @pl.loop(0, tiles.shape[0], step=PER)
        def _(start):
            for p in range(PER):
                store_edges(out[start + p], outer, inner, start + p)

    @pl.when(side[0] != 0)
    def _():
        @pl.loop(0, tiles.shape[0], step=PER)
        def _(start):
            for p in range(PER):
                store_edges(out[start + p], inner, outer, start + p)


def last_column_stage(side, tiles, near, far, table):
    count = tiles.shape[0]
    whole = jax.ShapeDtypeStruct((count, BANDS, ROWS, COLS), F32)
    edge = jax.ShapeDtypeStruct((count, BANDS * HALF, COLS), F32)
    return pl.pallas_call(
        last_column_kernel, out_shape=(whole, edge, edge, SIDE),
        in_specs=[SMEM] + [VMEM] * 4, out_specs=(VMEM, VMEM, VMEM, SMEM),
        compiler_params=params(), cost_estimate=cost(count * 4 * 2 * 256**3, count * 2**20),
        name="last_column_stage",
    )(side, tiles, near, far, table)


def sketch_kernel(side, tiles, inner, outer, matrix, signs, scale, out, after):
    hand_on(side, after)

    @pl.loop(0, out.shape[0], step=PER)
    def _(start):
        for p in range(PER):
            spot = start + p
            whole = jnp.concatenate(
                [stacked(tiles[spot].reshape(256, COLS)), stacked(halo_rows(outer, inner, spot))], axis=0
            )
            mixed = dot(matrix[...], whole).reshape(BANDS, ROWS, COLS)
            out[spot] = scale[...] * mixed + signed(signs[spot])


def sketch_stage(side, tiles, inner, outer, matrix, signs, scale):
    count = tiles.shape[0]
    return pl.pallas_call(
        sketch_kernel, out_shape=(jax.ShapeDtypeStruct((count, BANDS, ROWS, COLS), F32), SIDE),
        in_specs=[SMEM] + [VMEM] * 6, out_specs=(VMEM, SMEM),
        compiler_params=params(), cost_estimate=cost(count * 2 * 256 * 1536 * 256, count * 2**20),
        name="sketch_stage",
    )(side, tiles, inner, outer, matrix, signs, scale)


def gather_group(refs, g):
    return jnp.concatenate([r[:, g].reshape(-1, COLS) for r in refs], axis=0)


def same_place(shape):
    return lax.broadcasted_iota(jnp.int32, shape, 0) % 8 == lax.broadcasted_iota(jnp.int32, shape, 1) % 8


def spread_ones(shape, long_dim):
    long = lax.broadcasted_iota(jnp.int32, shape, long_dim) // 8
    short = lax.broadcasted_iota(jnp.int32, shape, 1 - long_dim)
    return (long == short).astype(F32)


def collapse(table):
    kept = jnp.where(same_place(table.shape), table, 0.0)
    rows, cols = table.shape
    return dot(dot(spread_ones((rows // 8, rows), 1), kept, HI), spread_ones((cols, cols // 8), 0), HI)


def early_gram_kernel(side, *refs):
    chunks, out, after, even, cross = refs[:-4], refs[-4], refs[-3], refs[-2], refs[-1]
    hand_on(side, after)
    even[...] = jnp.zeros_like(even)
    cross[...] = jnp.zeros_like(cross)

    @pl.loop(0, chunks[0].shape[1], step=8)
    def _(g):
        values = jnp.concatenate([gather_group(chunks, g + j) for j in range(8)], axis=1)
        high, low = split(values)
        even[...] += dot_nt(high, high) + dot_nt(low, low)
        cross[...] += dot_nt(high, low)

    mixed = collapse(cross[...])
    out[...] = collapse(even[...]) + (mixed + mixed.T)


def early_gram_stage(side, chunks):
    probes = sum(c.shape[0] for c in chunks)
    return pl.pallas_call(
        early_gram_kernel, out_shape=(jax.ShapeDtypeStruct((probes, probes), F32), SIDE),
        in_specs=[SMEM] + [VMEM] * len(chunks), out_specs=(VMEM, SMEM),
        scratch_shapes=[pltpu.VMEM((8 * probes, 8 * probes), F32)] * 2,
        compiler_params=params(), cost_estimate=cost(32 * 2 * 2 * 256**3, 2**23), name="early_gram_stage",
    )(side, *chunks)


def gram_kernel(early, *refs):
    chunks, out, total = refs[:-2], refs[-2], refs[-1]
    total[...] = jnp.zeros_like(total)
    done = early.shape[0]

    @pl.loop(0, chunks[0].shape[1], step=8)
    def _(g):
        values = jnp.concatenate([gather_group(chunks, g + j) for j in range(8)], axis=1)
        high, low = split(values)
        new_high, new_low = high[8 * done:], low[8 * done:]
        total[...] += dot_nt(jnp.concatenate([new_high, new_low], axis=0), high)
        total[...] += dot_nt(jnp.concatenate([new_low, new_high], axis=0), low)

    rows = total.shape[0] // 2
    late = collapse(total[0:rows] + total[rows:])
    corner = 0.5 * (late[:, done:] + late[:, done:].T)
    gram = jnp.concatenate(
        [
            jnp.concatenate([early[...], late[:, :done].T], axis=1),
            jnp.concatenate([late[:, :done], corner], axis=1),
        ],
        axis=0,
    )
    out[0] = jnp.concatenate([gram[8 * j:8 * j + 8] for j in range(4)], axis=1)
    out[1] = jnp.zeros(out.shape[1:], F32)


def gram_stage(early, chunks):
    probes = sum(c.shape[0] for c in chunks)
    return pl.pallas_call(
        gram_kernel, out_shape=jax.ShapeDtypeStruct((2, 8, 128), F32),
        in_specs=[VMEM] * (1 + len(chunks)), out_specs=VMEM,
        scratch_shapes=[pltpu.VMEM((16 * chunks[-1].shape[0], 8 * probes), F32)],
        compiler_params=params(), cost_estimate=cost(32 * 2 * 2 * 256**3, 2**23), name="gram_stage",
    )(early, *chunks)


def group_blocks(chunks):
    return [pl.BlockSpec((c.shape[0], PER, 8, COLS), lambda i: (0, i, 0, 0)) for c in chunks]


def two_sum(a, b):
    total = a + b
    part = total - a
    return total, (a - (total - part)) + (b - part)


def quick_sum(a, b):
    total = a + b
    return total, b - (total - a)


def halves(a):
    wide = a * 4097.0
    high = wide - (wide - a)
    return high, a - high


def two_product(a, b):
    product = a * b
    ah, al = halves(a)
    bh, bl = halves(b)
    return product, ((ah * bh - product) + ah * bl + al * bh) + al * bl


def pair_add(a, b):
    total, error = two_sum(a[0], b[0])
    return quick_sum(total, error + (a[1] + b[1]))


def pair_mul(a, b):
    product, error = two_product(a[0], b[0])
    return quick_sum(product, error + (a[0] * b[1] + a[1] * b[0]))


def pair_neg(a):
    return -a[0], -a[1]


def merge_kernel(mine, other, out):
    total = pair_add((mine[0], mine[1]), (other[0], other[1]))
    out[0] = total[0]
    out[1] = total[1]


def merge(mine, other):
    return pl.pallas_call(
        merge_kernel, out_shape=jax.ShapeDtypeStruct(mine.shape, F32),
        in_specs=[VMEM] * 2, out_specs=VMEM, compiler_params=params(), name="merge",
    )(mine, other)


def sum_over(value, axis):
    count = lax.axis_size(axis)
    bit = 1
    while bit < count:
        value = merge(value, lax.ppermute(value, axis, [(i, i ^ bit) for i in range(count)]))
        bit *= 2
    return value


def factor_kernel(gram, factor, inverse, work, *, norm):
    order = factor.shape[0]
    work[...] = jnp.zeros_like(work)
    row = lax.broadcasted_iota(jnp.int32, (order, 128), 0)
    lane = lax.broadcasted_iota(jnp.int32, (order, 128), 1)
    work[0] = (lane == row + order).astype(F32)
    for j in range(4):
        work[:, 8 * j:8 * j + 8, 0:order] = gram[:, :, j * order:(j + 1) * order]
    now = (work[0], work[1])
    for k in range(order - 1):
        pivot_row = tuple(v[k:k + 1, :] for v in now)
        pivot = tuple(jnp.broadcast_to(v[:, k:k + 1], (1, 128)) for v in pivot_row)
        first = pivot_row[0] / pivot[0]
        rest = pair_add(pivot_row, pair_neg(pair_mul((first, jnp.zeros_like(first)), pivot)))
        ratio = quick_sum(first, rest[0] / pivot[0])
        column = tuple(
            jnp.where(row > k, jnp.broadcast_to(v[:, k:k + 1], (order, 128)), 0.0) for v in now
        )
        now = pair_add(now, pair_neg(pair_mul(column, ratio)))
    diagonal = jnp.sum(jnp.where(lane == row, now[0], 0.0), axis=1, keepdims=True)
    scaled = now[0] / jnp.sqrt(diagonal)
    factor[...] = jnp.where(lane >= row, scaled, 0.0)[:, 0:order] * (1.0 / norm)
    inverse[...] = scaled[:, order:2 * order] * norm


def factor_stage(gram, order, norm):
    square = jax.ShapeDtypeStruct((order, order), F32)
    return pl.pallas_call(
        lambda *refs: factor_kernel(*refs, norm=norm), out_shape=(square, square),
        in_specs=[VMEM], out_specs=(VMEM, VMEM), scratch_shapes=[pltpu.VMEM((2, order, 128), F32)],
        compiler_params=params(), name="factor_stage",
    )(gram)


def basis_kernel(inverse, *refs):
    chunks, out, matrix = refs[:-2], refs[-2], refs[-1]
    order = matrix.shape[0]

    @pl.when(pl.program_id(0) == 0)
    def _():
        wide = dot(dot(spread_ones((order, order // 8), 0), inverse[...], HI), spread_ones((order // 8, order), 1), HI)
        high, low = split(jnp.where(same_place((order, order)), wide, 0.0))
        matrix[:, 0:order] = high
        matrix[:, order:2 * order] = low
        matrix[:, 2 * order:3 * order] = high

    start = pl.program_id(0) * out.shape[1]
    for g in range(out.shape[1]):
        values = dot(matrix[...], stacked(gather_group(chunks, start + g)))
        out[:, g] = values.reshape(-1, 8, COLS)


def basis_stage(inverse, chunks):
    probes = inverse.shape[0]
    groups = chunks[0].shape[1]
    return pl.pallas_call(
        basis_kernel, grid=(groups // 8,),
        out_shape=jax.ShapeDtypeStruct((probes, groups, 8, COLS), F32),
        in_specs=[VMEM] * (1 + len(chunks)),
        out_specs=pl.BlockSpec((probes, 8, 8, COLS), lambda i: (0, i, 0, 0)),
        scratch_shapes=[pltpu.VMEM((256, 768), BF16)],
        compiler_params=params(), cost_estimate=cost(32 * 3 * 2 * 256**3, 2**24), name="basis_stage",
    )(inverse, *chunks)


def swap(inner, outer, axis):
    count = lax.axis_size(axis)
    pairs = [(i, i ^ 1) for i in range(count)]
    others = [p for i in range(1, count - 1, 2) for p in ((i, i + 1), (i + 1, i))]
    return lax.ppermute(inner, axis, pairs), lax.ppermute(outer, axis, others)


def shards(probe_signs, prior_scale, prior_factor, band_mix, inverse_noise_variance):
    probes = probe_signs.shape[0]
    side = jnp.stack([lax.axis_index("row") % 2, lax.axis_index("col") % 2]).astype(jnp.int32)
    table = jnp.asarray(col_constants())
    starts = [sum(CHUNKS[:k]) for k in range(len(CHUNKS))]
    signs = [probe_signs[start:start + count] for start, count in zip(starts, CHUNKS)]
    rows = [swap(*edges(side, part, prior_scale), "row") for part in signs]
    first_m, last_m, mix_m, back_m = prepare(side, prior_factor, band_mix)
    last = len(CHUNKS) - 1
    state = {}

    def first(k, side):
        *state[k], side = first_stage(side, signs[k], prior_scale, *rows[k], first_m)
        state[k][1:] = swap(*state[k][1:], "col")
        return side

    def middle(k, side, ahead=None):
        *state[k], side = middle_stage(side, *state[k], table, mix_m, back_m, inverse_noise_variance, ahead)
        state[k][1:] = swap(*state[k][1:], "col")
        return side

    def last_column(k, side):
        *state[k], side = last_column_stage(side, *state[k], table)
        state[k][1:] = swap(*state[k][1:], "row")
        return side

    def finish(k, side):
        state[k], side = sketch_stage(side, *state[k], last_m, signs[k], prior_scale)
        return side

    def group(k):
        return state[k].reshape(CHUNKS[k], BANDS * ROWS // 8, 8, COLS)

    side = first(0, side)
    side = middle(0, side)
    side = first(1, side)
    side = last_column(0, side)
    for k in range(2, last + 1):
        side = middle(k - 1, side, state[k - 2][1])
        side = first(k, side)
        side = last_column(k - 1, side)
    side = middle(last, side, state[last - 1][1])
    for k in range(last - 1):
        side = finish(k, side)
    side = last_column(last, side)
    side = finish(last - 1, side)
    early, side = early_gram_stage(side, [group(k) for k in range(last)])
    side = finish(last, side)
    grouped = [group(k) for k in range(last + 1)]
    gram = sum_over(sum_over(gram_stage(early, grouped), "row"), "col")
    total = BANDS * ROWS * COLS * lax.axis_size("row") * lax.axis_size("col")
    r_factor, inverse = factor_stage(gram, probes, float(np.sqrt(np.float32(total))))
    basis = basis_stage(inverse, grouped)
    return basis.reshape(probes, BANDS, ROWS, COLS), r_factor


def solution(mesh):
    in_specs = (P(None, None, "row", "col"), P(None, "row", "col"), P(), P(), P(None, "row", "col"))
    out_specs = (P(None, None, "row", "col"), P())
    return jax.shard_map(shards, mesh=mesh, in_specs=in_specs, out_specs=out_specs, check_vma=False)
```

```python
import numpy as np
import jax
import jax.numpy as jnp
from jax import lax
from jax.experimental import pallas as pl
from jax.experimental.pallas import tpu as pltpu
from jax.sharding import PartitionSpec as P

BANDS = 8
HALF = 15
TAPS = 31
ROWS = 32
COLS = 256
CHUNKS = (8, 12, 12)
PER = 4

F32 = jnp.float32
BF16 = jnp.bfloat16
HI = lax.Precision.HIGHEST
VMEM = pl.BlockSpec(memory_space=pltpu.VMEM)
SMEM = pl.BlockSpec(memory_space=pltpu.SMEM)
SIDE = jax.ShapeDtypeStruct((2,), jnp.int32)


def taps_np():
    offsets = np.arange(TAPS) - HALF
    sigma = 1.0 + 0.5 * np.arange(BANDS)
    raw = np.exp(-offsets[None, :] ** 2 / (2.0 * sigma[:, None] ** 2))
    return raw / raw.sum(axis=1, keepdims=True)


def table_np(pos_in, pos_out):
    taps = taps_np()
    offset = np.asarray(pos_in)[:, None] - np.asarray(pos_out)[None, :]
    inside = np.abs(offset) <= HALF
    return np.where(inside[None], taps[:, np.clip(offset + HALF, 0, TAPS - 1)], 0.0)


def split_np(values):
    high = values.astype(BF16)
    low = (values - high.astype(np.float64)).astype(BF16)
    return high, low


def row_constants():
    out = np.arange(ROWS)
    main = table_np(np.arange(ROWS), out)
    above = table_np(np.arange(-HALF, 0), out)
    below = table_np(np.arange(ROWS, ROWS + HALF), out)
    by_out = np.zeros((BANDS, ROWS, 512))
    by_in = np.zeros((BANDS, ROWS, 512))
    pick = np.zeros((BANDS, 512))
    for c in range(BANDS):
        parts = ((c * ROWS, ROWS, main), (256 + c * HALF, HALF, above), (376 + c * HALF, HALF, below))
        for start, size, table in parts:
            by_out[:, :, start:start + size] = table.transpose(0, 2, 1)
            by_in[:, :, start:start + size] = table[c].T[None]
            pick[c, start:start + size] = 1.0
    spread = np.repeat(np.eye(BANDS), ROWS, axis=0)
    same = np.tile(np.eye(ROWS), (BANDS, BANDS))
    return [v.astype(np.float32) for v in (by_out.reshape(256, 512), by_in.reshape(256, 512), pick, spread, same)]


def col_constants():
    out = np.arange(COLS)
    main = table_np(np.arange(COLS), out)
    left = table_np(np.arange(-16, 0), out)
    right = table_np(np.arange(COLS, COLS + 16), out)
    main_h, main_l = split_np(main)
    halo_h, halo_l = split_np(np.concatenate([left, right], axis=1))
    halo = np.zeros((BANDS, 256, COLS), BF16)
    halo[:, 0:32] = halo_h
    halo[:, 32:64] = halo_l
    halo[:, 128:160] = halo_h
    return np.concatenate([main_h, main_h, main_l, halo], axis=1)


def split(values):
    high = values.astype(BF16)
    return high, (values - high.astype(F32)).astype(BF16)


def dot(a, b, precision=None):
    return lax.dot_general(a, b, (((1,), (0,)), ((), ())), precision=precision, preferred_element_type=F32)


def dot_nt(a, b):
    return lax.dot_general(a, b, (((1,), (1,)), ((), ())), preferred_element_type=F32)


def stacked(values):
    high, low = split(values)
    return jnp.concatenate([high, high, low], axis=0)


def hand_on(side, after):
    after[0] = side[0]
    after[1] = side[1]


def params(mib=20):
    return pltpu.CompilerParams(vmem_limit_bytes=mib * 2**20)


def cost(flops, moved):
    return pl.CostEstimate(flops=int(flops), bytes_accessed=int(moved), transcendentals=0)


def prepare_kernel(side, factor, mix, by_out, by_in, pick, spread, same, first_m, last_m, mix_m, back_m):
    lower = side[0] == 0
    def expand(small, right):
        return dot(dot(spread[...], small, HI), right, HI)

    def store(out, whole):
        for part in range(whole.shape[1] // 256):
            high, low = split(whole[:, part * 256:part * 256 + 256])
            out[:, part * 768:part * 768 + 256] = high
            out[:, part * 768 + 256:part * 768 + 512] = low
            out[:, part * 768 + 512:part * 768 + 768] = high

    f = factor[...]
    a = mix[...]

    def ordered(table):
        whole = table[...]
        above, below, rest = whole[:, 256:376], whole[:, 376:496], whole[:, 496:512]
        swapped = jnp.concatenate([whole[:, 0:256], below, above, rest], axis=1)
        return jnp.where(lower, whole, swapped)

    store(first_m, expand(f, pick[...]) * ordered(by_out))
    store(last_m, expand(f.T, pick[...]) * ordered(by_in))
    store(mix_m, expand(a, pick[:, :256]) * same[...])
    store(back_m, expand(a.T, pick[:, :256]) * same[...])


def prepare(side, factor, mix):
    wide = jax.ShapeDtypeStruct((256, 1536), BF16)
    narrow = jax.ShapeDtypeStruct((256, 768), BF16)
    return pl.pallas_call(
        prepare_kernel, out_shape=(wide, wide, narrow, narrow),
        in_specs=[SMEM] + [VMEM] * 7, out_specs=(VMEM,) * 4, compiler_params=params(),
        name="prepare",
    )(side, factor, mix, *[jnp.asarray(v) for v in row_constants()])


def signed(ref_value):
    return 2.0 * ref_value.astype(F32) - 1.0


def store_edges(tile, top, bottom, p):
    for b in range(BANDS):
        top[p, b * HALF:(b + 1) * HALF, :] = tile[b, 0:HALF, :]
        bottom[p, b * HALF:(b + 1) * HALF, :] = tile[b, ROWS - HALF:ROWS, :]


def store_by_side(tile, lower, inner, outer, p):
    @pl.when(lower)
    def _():
        store_edges(tile, outer, inner, p)

    @pl.when(jnp.logical_not(lower))
    def _():
        store_edges(tile, inner, outer, p)


def edge_kernel(side, signs, scale, inner, outer):
    for p in range(signs.shape[0]):
        store_by_side(scale[...] * signed(signs[p]), side[0] == 0, inner, outer, p)


def edges(side, signs, scale):
    count = signs.shape[0]
    shape = jax.ShapeDtypeStruct((count, BANDS * HALF, COLS), F32)
    return pl.pallas_call(
        edge_kernel, grid=(count // PER,), out_shape=(shape, shape),
        in_specs=[
            SMEM,
            pl.BlockSpec((PER, BANDS, ROWS, COLS), lambda i: (i, 0, 0, 0)),
            pl.BlockSpec((BANDS, ROWS, COLS), lambda i: (0, 0, 0)),
        ],
        out_specs=[pl.BlockSpec((PER, BANDS * HALF, COLS), lambda i: (i, 0, 0))] * 2,
        compiler_params=params(), cost_estimate=cost(1e6, count * 2**19), name="edges",
    )(side, signs, scale)


def store_packed(tile, lower, near, far, p):
    lane = lax.broadcasted_iota(jnp.int32, (ROWS, 128), 1) // 16
    low = tile[0, :, :128]
    high = pltpu.roll(tile[0, :, 128:], 16, 1)
    for b in range(1, BANDS):
        low = jnp.where(lane == b, pltpu.roll(tile[b, :, :128], 16 * b, 1), low)
        mine = tile[b, :, 128:]
        if b < BANDS - 1:
            mine = pltpu.roll(mine, 16 * b + 16, 1)
        high = jnp.where(lane == b, mine, high)
    near[p] = jnp.where(lower, high, low)
    far[p] = jnp.where(lower, low, high)


def halo_rows(outer, inner, p):
    return jnp.concatenate([outer[p], inner[p], jnp.zeros((16, COLS), F32)], axis=0)


def first_kernel(side, signs, scale, inner, outer, matrix, out, near, far, after):
    hand_on(side, after)

    @pl.loop(0, out.shape[0], step=PER)
    def _(start):
        for p in range(PER):
            scaled = (scale[...] * signed(signs[start + p])).reshape(256, COLS)
            whole = jnp.concatenate([stacked(scaled), stacked(halo_rows(outer, inner, start + p))], axis=0)
            tile = dot(matrix[...], whole).reshape(BANDS, ROWS, COLS)
            out[start + p] = tile
            store_packed(tile, side[1] == 0, near, far, start + p)


def first_stage(side, signs, scale, inner, outer, matrix):
    count = signs.shape[0]
    packed = jax.ShapeDtypeStruct((count, ROWS, 128), F32)
    return pl.pallas_call(
        first_kernel,
        out_shape=(jax.ShapeDtypeStruct((count, BANDS, ROWS, COLS), F32), packed, packed, SIDE),
        in_specs=[SMEM] + [VMEM] * 5, out_specs=(VMEM, VMEM, VMEM, SMEM),
        compiler_params=params(), cost_estimate=cost(count * 2 * 256 * 1536 * 256, count * 2**20),
        name="first_stage",
    )(side, signs, scale, inner, outer, matrix)


def column_blur(lower, tiles, near, far, table, out):
    count = tiles.shape[0]
    flat = count * ROWS
    first = near[...].reshape(flat, 128)
    other = far[...].reshape(flat, 128)
    left = jnp.where(lower, other, first)
    right = jnp.where(lower, first, other)
    lane = lax.broadcasted_iota(jnp.int32, (flat, 128), 1)

    @pl.loop(0, BANDS, step=4)
    def _(start):
        for b in [start + j for j in range(4)]:
            uh, ul = split(tiles[:, b].reshape(flat, COLS))
            sides = jnp.where(lane < 16, pltpu.roll(left, 128 - 16 * b, 1), pltpu.roll(right, (144 - 16 * b) % 128, 1))
            sides = jnp.where(lane < 32, sides, pltpu.roll(sides, 32, 1))
            eh, el = split(sides)
            blurred = dot(jnp.concatenate([uh, ul, uh, eh, el], axis=1), table[b])
            out[:, b] = blurred.reshape(count, ROWS, COLS)


def middle_kernel(side, tiles, near, far, table, mix, back, weights, ahead, out, out_near, out_far, after, blurred):
    hand_on(side, after)
    lower = side[1] == 0
    column_blur(lower, tiles, near, far, table, blurred)
    weight = weights[...].reshape(256, COLS)

    group = 6 if tiles.shape[0] % 6 == 0 else 8

    @pl.loop(0, tiles.shape[0], step=group)
    def _(start):
        for p in range(group):
            weighted = weight * dot(mix[...], stacked(blurred[start + p].reshape(256, COLS)))
            tile = dot(back[...], stacked(weighted)).reshape(BANDS, ROWS, COLS)
            out[start + p] = tile
            store_packed(tile, lower, out_near, out_far, start + p)


def middle_stage(side, tiles, near, far, table, mix, back, weights, ahead):
    ahead = side if ahead is None else ahead
    count = tiles.shape[0]
    whole = jax.ShapeDtypeStruct((count, BANDS, ROWS, COLS), F32)
    packed = jax.ShapeDtypeStruct((count, ROWS, 128), F32)
    return pl.pallas_call(
        middle_kernel, out_shape=(whole, packed, packed, SIDE),
        in_specs=[SMEM] + [VMEM] * 7 + [pl.BlockSpec(memory_space=pl.ANY)], out_specs=(VMEM, VMEM, VMEM, SMEM),
        scratch_shapes=[pltpu.VMEM((count, BANDS, ROWS, COLS), F32)],
        compiler_params=params(), cost_estimate=cost(count * 10 * 2 * 256**3, count * 2**20),
        name="middle_stage",
    )(side, tiles, near, far, table, mix, back, weights, ahead)


def last_column_kernel(side, tiles, near, far, table, out, inner, outer, after):
    hand_on(side, after)
    column_blur(side[1] == 0, tiles, near, far, table, out)

    @pl.when(side[0] == 0)
    def _():
        @pl.loop(0, tiles.shape[0], step=PER)
        def _(start):
            for p in range(PER):
                store_edges(out[start + p], outer, inner, start + p)

    @pl.when(side[0] != 0)
    def _():
        @pl.loop(0, tiles.shape[0], step=PER)
        def _(start):
            for p in range(PER):
                store_edges(out[start + p], inner, outer, start + p)


def last_column_stage(side, tiles, near, far, table):
    count = tiles.shape[0]
    whole = jax.ShapeDtypeStruct((count, BANDS, ROWS, COLS), F32)
    edge = jax.ShapeDtypeStruct((count, BANDS * HALF, COLS), F32)
    return pl.pallas_call(
        last_column_kernel, out_shape=(whole, edge, edge, SIDE),
        in_specs=[SMEM] + [VMEM] * 4, out_specs=(VMEM, VMEM, VMEM, SMEM),
        compiler_params=params(), cost_estimate=cost(count * 4 * 2 * 256**3, count * 2**20),
        name="last_column_stage",
    )(side, tiles, near, far, table)


def sketch_kernel(side, tiles, inner, outer, matrix, signs, scale, out, after):
    hand_on(side, after)

    @pl.loop(0, out.shape[0], step=PER)
    def _(start):
        for p in range(PER):
            spot = start + p
            whole = jnp.concatenate(
                [stacked(tiles[spot].reshape(256, COLS)), stacked(halo_rows(outer, inner, spot))], axis=0
            )
            mixed = dot(matrix[...], whole).reshape(BANDS, ROWS, COLS)
            out[spot] = scale[...] * mixed + signed(signs[spot])


def sketch_stage(side, tiles, inner, outer, matrix, signs, scale):
    count = tiles.shape[0]
    return pl.pallas_call(
        sketch_kernel, out_shape=(jax.ShapeDtypeStruct((count, BANDS, ROWS, COLS), F32), SIDE),
        in_specs=[SMEM] + [VMEM] * 6, out_specs=(VMEM, SMEM),
        compiler_params=params(), cost_estimate=cost(count * 2 * 256 * 1536 * 256, count * 2**20),
        name="sketch_stage",
    )(side, tiles, inner, outer, matrix, signs, scale)


def sketch_main_kernel(side, tiles, matrix, out, after):
    hand_on(side, after)

    @pl.loop(0, out.shape[0], step=PER)
    def _(start):
        for p in range(PER):
            out[start + p] = dot(matrix[:, 0:768], stacked(tiles[start + p].reshape(256, COLS)))


def sketch_main_stage(side, tiles, matrix):
    count = tiles.shape[0]
    return pl.pallas_call(
        sketch_main_kernel, out_shape=(jax.ShapeDtypeStruct((count, 256, COLS), F32), SIDE),
        in_specs=[SMEM, VMEM, VMEM], out_specs=(VMEM, SMEM),
        compiler_params=params(), cost_estimate=cost(count * 256 * 1536 * 256, count * 2**19),
        name="sketch_main_stage",
    )(side, tiles, matrix)


def gather_group(refs, g):
    return jnp.concatenate([r[:, g].reshape(-1, COLS) for r in refs], axis=0)


def same_place(shape):
    return lax.broadcasted_iota(jnp.int32, shape, 0) % 8 == lax.broadcasted_iota(jnp.int32, shape, 1) % 8


def spread_ones(shape, long_dim):
    long = lax.broadcasted_iota(jnp.int32, shape, long_dim) // 8
    short = lax.broadcasted_iota(jnp.int32, shape, 1 - long_dim)
    return (long == short).astype(F32)


def collapse(table):
    kept = jnp.where(same_place(table.shape), table, 0.0)
    rows, cols = table.shape
    return dot(dot(spread_ones((rows // 8, rows), 1), kept, HI), spread_ones((cols, cols // 8), 0), HI)


def early_gram_kernel(side, *refs):
    chunks, out, after, even, cross = refs[:-4], refs[-4], refs[-3], refs[-2], refs[-1]
    hand_on(side, after)
    even[...] = jnp.zeros_like(even)
    cross[...] = jnp.zeros_like(cross)

    @pl.loop(0, chunks[0].shape[1], step=8)
    def _(g):
        values = jnp.concatenate([gather_group(chunks, g + j) for j in range(8)], axis=1)
        high, low = split(values)
        even[...] += dot_nt(high, high) + dot_nt(low, low)
        cross[...] += dot_nt(high, low)

    mixed = collapse(cross[...])
    out[...] = collapse(even[...]) + (mixed + mixed.T)


def early_gram_stage(side, chunks):
    probes = sum(c.shape[0] for c in chunks)
    return pl.pallas_call(
        early_gram_kernel, out_shape=(jax.ShapeDtypeStruct((probes, probes), F32), SIDE),
        in_specs=[SMEM] + [VMEM] * len(chunks), out_specs=(VMEM, SMEM),
        scratch_shapes=[pltpu.VMEM((8 * probes, 8 * probes), F32)] * 2,
        compiler_params=params(), cost_estimate=cost(32 * 2 * 2 * 256**3, 2**23), name="early_gram_stage",
    )(side, *chunks)


def gram_kernel(early, main, inner, outer, matrix, signs, scale, *refs):
    chunks, out, sketch, total = refs[:-3], refs[-3], refs[-2], refs[-1]
    total[...] = jnp.zeros_like(total)
    done = early.shape[0]

    @pl.loop(0, main.shape[0], step=PER)
    def _(start):
        for p in range(PER):
            spot = start + p
            mixed = main[spot] + dot(matrix[:, 768:], stacked(halo_rows(outer, inner, spot)))
            values = scale[...] * mixed.reshape(BANDS, ROWS, COLS) + signed(signs[spot])
            sketch[spot] = values.reshape(BANDS * ROWS // 8, 8, COLS)

    whole = chunks + (sketch,)

    @pl.loop(0, sketch.shape[1], step=8)
    def _(g):
        values = jnp.concatenate([gather_group(whole, g + j) for j in range(8)], axis=1)
        high, low = split(values)
        new_high, new_low = high[8 * done:], low[8 * done:]
        total[...] += dot_nt(jnp.concatenate([new_high, new_low], axis=0), high)
        total[...] += dot_nt(jnp.concatenate([new_low, new_high], axis=0), low)

    rows = total.shape[0] // 2
    late = collapse(total[0:rows] + total[rows:])
    corner = 0.5 * (late[:, done:] + late[:, done:].T)
    gram = jnp.concatenate(
        [
            jnp.concatenate([early[...], late[:, :done].T], axis=1),
            jnp.concatenate([late[:, :done], corner], axis=1),
        ],
        axis=0,
    )
    out[0] = jnp.concatenate([gram[8 * j:8 * j + 8] for j in range(4)], axis=1)
    out[1] = jnp.zeros(out.shape[1:], F32)


def gram_stage(early, main, inner, outer, matrix, signs, scale, chunks):
    count = main.shape[0]
    probes = sum(c.shape[0] for c in chunks) + count
    grouped = jax.ShapeDtypeStruct((count, BANDS * ROWS // 8, 8, COLS), F32)
    return pl.pallas_call(
        gram_kernel, out_shape=(jax.ShapeDtypeStruct((2, 8, 128), F32), grouped),
        in_specs=[VMEM] * (7 + len(chunks)), out_specs=(VMEM, VMEM),
        scratch_shapes=[pltpu.VMEM((16 * count, 8 * probes), F32)],
        compiler_params=params(), cost_estimate=cost(32 * 2 * 2 * 256**3, 2**23), name="gram_stage",
    )(early, main, inner, outer, matrix, signs, scale, *chunks)


def group_blocks(chunks):
    return [pl.BlockSpec((c.shape[0], PER, 8, COLS), lambda i: (0, i, 0, 0)) for c in chunks]


def two_sum(a, b):
    total = a + b
    part = total - a
    return total, (a - (total - part)) + (b - part)


def quick_sum(a, b):
    total = a + b
    return total, b - (total - a)


def halves(a):
    wide = a * 4097.0
    high = wide - (wide - a)
    return high, a - high


def two_product(a, b):
    product = a * b
    ah, al = halves(a)
    bh, bl = halves(b)
    return product, ((ah * bh - product) + ah * bl + al * bh) + al * bl


def pair_add(a, b):
    total, error = two_sum(a[0], b[0])
    return quick_sum(total, error + (a[1] + b[1]))


def pair_mul(a, b):
    product, error = two_product(a[0], b[0])
    return quick_sum(product, error + (a[0] * b[1] + a[1] * b[0]))


def pair_neg(a):
    return -a[0], -a[1]


def merge_kernel(mine, other, out):
    total = pair_add((mine[0], mine[1]), (other[0], other[1]))
    out[0] = total[0]
    out[1] = total[1]


def merge(mine, other):
    return pl.pallas_call(
        merge_kernel, out_shape=jax.ShapeDtypeStruct(mine.shape, F32),
        in_specs=[VMEM] * 2, out_specs=VMEM, compiler_params=params(), name="merge",
    )(mine, other)


def sum_over(value, axis):
    count = lax.axis_size(axis)
    bit = 1
    while bit < count:
        value = merge(value, lax.ppermute(value, axis, [(i, i ^ bit) for i in range(count)]))
        bit *= 2
    return value


def factor_kernel(gram, factor, inverse, work, *, norm):
    order = factor.shape[0]
    work[...] = jnp.zeros_like(work)
    row = lax.broadcasted_iota(jnp.int32, (order, 128), 0)
    lane = lax.broadcasted_iota(jnp.int32, (order, 128), 1)
    work[0] = (lane == row + order).astype(F32)
    for j in range(4):
        work[:, 8 * j:8 * j + 8, 0:order] = gram[:, :, j * order:(j + 1) * order]
    now = (work[0], work[1])
    for k in range(order - 1):
        pivot_row = tuple(v[k:k + 1, :] for v in now)
        pivot = tuple(jnp.broadcast_to(v[:, k:k + 1], (1, 128)) for v in pivot_row)
        first = pivot_row[0] / pivot[0]
        rest = pair_add(pivot_row, pair_neg(pair_mul((first, jnp.zeros_like(first)), pivot)))
        ratio = quick_sum(first, rest[0] / pivot[0])
        column = tuple(
            jnp.where(row > k, jnp.broadcast_to(v[:, k:k + 1], (order, 128)), 0.0) for v in now
        )
        now = pair_add(now, pair_neg(pair_mul(column, ratio)))
    diagonal = jnp.sum(jnp.where(lane == row, now[0], 0.0), axis=1, keepdims=True)
    scaled = now[0] / jnp.sqrt(diagonal)
    factor[...] = jnp.where(lane >= row, scaled, 0.0)[:, 0:order] * (1.0 / norm)
    inverse[...] = scaled[:, order:2 * order] * norm


def factor_stage(gram, order, norm):
    square = jax.ShapeDtypeStruct((order, order), F32)
    return pl.pallas_call(
        lambda *refs: factor_kernel(*refs, norm=norm), out_shape=(square, square),
        in_specs=[VMEM], out_specs=(VMEM, VMEM), scratch_shapes=[pltpu.VMEM((2, order, 128), F32)],
        compiler_params=params(), name="factor_stage",
    )(gram)


def basis_kernel(inverse, *refs):
    chunks, out, matrix = refs[:-2], refs[-2], refs[-1]
    order = matrix.shape[0]

    @pl.when(pl.program_id(0) == 0)
    def _():
        wide = dot(dot(spread_ones((order, order // 8), 0), inverse[...], HI), spread_ones((order // 8, order), 1), HI)
        high, low = split(jnp.where(same_place((order, order)), wide, 0.0))
        matrix[:, 0:order] = high
        matrix[:, order:2 * order] = low
        matrix[:, 2 * order:3 * order] = high

    start = pl.program_id(0) * out.shape[1]
    for g in range(out.shape[1]):
        values = dot(matrix[...], stacked(gather_group(chunks, start + g)))
        out[:, g] = values.reshape(-1, 8, COLS)


def basis_stage(inverse, chunks):
    probes = inverse.shape[0]
    groups = chunks[0].shape[1]
    return pl.pallas_call(
        basis_kernel, grid=(groups // 8,),
        out_shape=jax.ShapeDtypeStruct((probes, groups, 8, COLS), F32),
        in_specs=[VMEM] * (1 + len(chunks)),
        out_specs=pl.BlockSpec((probes, 8, 8, COLS), lambda i: (0, i, 0, 0)),
        scratch_shapes=[pltpu.VMEM((256, 768), BF16)],
        compiler_params=params(), cost_estimate=cost(32 * 3 * 2 * 256**3, 2**24), name="basis_stage",
    )(inverse, *chunks)


def swap(inner, outer, axis):
    count = lax.axis_size(axis)
    pairs = [(i, i ^ 1) for i in range(count)]
    others = [p for i in range(1, count - 1, 2) for p in ((i, i + 1), (i + 1, i))]
    return lax.ppermute(inner, axis, pairs), lax.ppermute(outer, axis, others)


def shards(probe_signs, prior_scale, prior_factor, band_mix, inverse_noise_variance):
    probes = probe_signs.shape[0]
    side = jnp.stack([lax.axis_index("row") % 2, lax.axis_index("col") % 2]).astype(jnp.int32)
    table = jnp.asarray(col_constants())
    starts = [sum(CHUNKS[:k]) for k in range(len(CHUNKS))]
    signs = [probe_signs[start:start + count] for start, count in zip(starts, CHUNKS)]
    rows = [swap(*edges(side, part, prior_scale), "row") for part in signs]
    first_m, last_m, mix_m, back_m = prepare(side, prior_factor, band_mix)
    last = len(CHUNKS) - 1
    state = {}

    def first(k, side):
        *state[k], side = first_stage(side, signs[k], prior_scale, *rows[k], first_m)
        state[k][1:] = swap(*state[k][1:], "col")
        return side

    def middle(k, side, ahead=None):
        *state[k], side = middle_stage(side, *state[k], table, mix_m, back_m, inverse_noise_variance, ahead)
        state[k][1:] = swap(*state[k][1:], "col")
        return side

    def last_column(k, side):
        *state[k], side = last_column_stage(side, *state[k], table)
        state[k][1:] = swap(*state[k][1:], "row")
        return side

    def finish(k, side):
        state[k], side = sketch_stage(side, *state[k], last_m, signs[k], prior_scale)
        return side

    def group(k):
        return state[k].reshape(CHUNKS[k], BANDS * ROWS // 8, 8, COLS)

    side = first(0, side)
    side = middle(0, side)
    side = first(1, side)
    side = last_column(0, side)
    for k in range(2, last + 1):
        side = middle(k - 1, side, state[k - 2][1])
        side = first(k, side)
        side = last_column(k - 1, side)
    side = middle(last, side, state[last - 1][1])
    for k in range(last - 1):
        side = finish(k, side)
    side = last_column(last, side)
    side = finish(last - 1, side)
    grouped = [group(k) for k in range(last)]
    early, side = early_gram_stage(side, grouped)
    tiles, *edge_rows = state[last]
    main, side = sketch_main_stage(side, tiles, last_m)
    gram, latest = gram_stage(early, main, *edge_rows, last_m, signs[last], prior_scale, grouped)
    grouped.append(latest)
    gram = sum_over(sum_over(gram, "row"), "col")
    total = BANDS * ROWS * COLS * lax.axis_size("row") * lax.axis_size("col")
    r_factor, inverse = factor_stage(gram, probes, float(np.sqrt(np.float32(total))))
    basis = basis_stage(inverse, grouped)
    return basis.reshape(probes, BANDS, ROWS, COLS), r_factor


def solution(mesh):
    in_specs = (P(None, None, "row", "col"), P(None, "row", "col"), P(), P(), P(None, "row", "col"))
    out_specs = (P(None, None, "row", "col"), P())
    return jax.shard_map(shards, mesh=mesh, in_specs=in_specs, out_specs=out_specs, check_vma=False)
```

```python
import numpy as np
import jax
import jax.numpy as jnp
from jax import lax
from jax.experimental import pallas as pl
from jax.experimental.pallas import tpu as pltpu
from jax.sharding import PartitionSpec as P

BANDS = 8
HALF = 15
TAPS = 31
ROWS = 32
COLS = 256
CHUNKS = (8, 12, 12)
PER = 4

F32 = jnp.float32
BF16 = jnp.bfloat16
HI = lax.Precision.HIGHEST
VMEM = pl.BlockSpec(memory_space=pltpu.VMEM)
SMEM = pl.BlockSpec(memory_space=pltpu.SMEM)
SIDE = jax.ShapeDtypeStruct((2,), jnp.int32)


def taps_np():
    offsets = np.arange(TAPS) - HALF
    sigma = 1.0 + 0.5 * np.arange(BANDS)
    raw = np.exp(-offsets[None, :] ** 2 / (2.0 * sigma[:, None] ** 2))
    return raw / raw.sum(axis=1, keepdims=True)


def table_np(pos_in, pos_out):
    taps = taps_np()
    offset = np.asarray(pos_in)[:, None] - np.asarray(pos_out)[None, :]
    inside = np.abs(offset) <= HALF
    return np.where(inside[None], taps[:, np.clip(offset + HALF, 0, TAPS - 1)], 0.0)


def split_np(values):
    high = values.astype(BF16)
    low = (values - high.astype(np.float64)).astype(BF16)
    return high, low


def row_constants():
    out = np.arange(ROWS)
    main = table_np(np.arange(ROWS), out)
    above = table_np(np.arange(-HALF, 0), out)
    below = table_np(np.arange(ROWS, ROWS + HALF), out)
    by_out = np.zeros((BANDS, ROWS, 512))
    by_in = np.zeros((BANDS, ROWS, 512))
    pick = np.zeros((BANDS, 512))
    for c in range(BANDS):
        parts = ((c * ROWS, ROWS, main), (256 + c * HALF, HALF, above), (376 + c * HALF, HALF, below))
        for start, size, table in parts:
            by_out[:, :, start:start + size] = table.transpose(0, 2, 1)
            by_in[:, :, start:start + size] = table[c].T[None]
            pick[c, start:start + size] = 1.0
    spread = np.repeat(np.eye(BANDS), ROWS, axis=0)
    same = np.tile(np.eye(ROWS), (BANDS, BANDS))
    return [v.astype(np.float32) for v in (by_out.reshape(256, 512), by_in.reshape(256, 512), pick, spread, same)]


def col_constants():
    out = np.arange(COLS)
    main = table_np(np.arange(COLS), out)
    left = table_np(np.arange(-16, 0), out)
    right = table_np(np.arange(COLS, COLS + 16), out)
    main_h, main_l = split_np(main)
    halo_h, halo_l = split_np(np.concatenate([left, right], axis=1))
    halo = np.zeros((BANDS, 256, COLS), BF16)
    halo[:, 0:32] = halo_h
    halo[:, 32:64] = halo_l
    halo[:, 128:160] = halo_h
    return np.concatenate([main_h, main_h, main_l, halo], axis=1)


def split(values):
    high = values.astype(BF16)
    return high, (values - high.astype(F32)).astype(BF16)


def dot(a, b, precision=None):
    return lax.dot_general(a, b, (((1,), (0,)), ((), ())), precision=precision, preferred_element_type=F32)


def dot_nt(a, b):
    return lax.dot_general(a, b, (((1,), (1,)), ((), ())), preferred_element_type=F32)


def stacked(values):
    high, low = split(values)
    return jnp.concatenate([high, high, low], axis=0)


def hand_on(side, after):
    after[0] = side[0]
    after[1] = side[1]


def params(mib=20):
    return pltpu.CompilerParams(vmem_limit_bytes=mib * 2**20)


def cost(flops, moved):
    return pl.CostEstimate(flops=int(flops), bytes_accessed=int(moved), transcendentals=0)


def prepare_kernel(side, factor, mix, by_out, by_in, pick, spread, same, first_m, last_m, mix_m, back_m):
    lower = side[0] == 0
    def expand(small, right):
        return dot(dot(spread[...], small, HI), right, HI)

    def store(out, whole):
        for part in range(whole.shape[1] // 256):
            high, low = split(whole[:, part * 256:part * 256 + 256])
            out[:, part * 768:part * 768 + 256] = high
            out[:, part * 768 + 256:part * 768 + 512] = low
            out[:, part * 768 + 512:part * 768 + 768] = high

    f = factor[...]
    a = mix[...]

    def ordered(table):
        whole = table[...]
        above, below, rest = whole[:, 256:376], whole[:, 376:496], whole[:, 496:512]
        swapped = jnp.concatenate([whole[:, 0:256], below, above, rest], axis=1)
        return jnp.where(lower, whole, swapped)

    store(first_m, expand(f, pick[...]) * ordered(by_out))
    store(last_m, expand(f.T, pick[...]) * ordered(by_in))
    store(mix_m, expand(a, pick[:, :256]) * same[...])
    store(back_m, expand(a.T, pick[:, :256]) * same[...])


def prepare(side, factor, mix):
    wide = jax.ShapeDtypeStruct((256, 1536), BF16)
    narrow = jax.ShapeDtypeStruct((256, 768), BF16)
    return pl.pallas_call(
        prepare_kernel, out_shape=(wide, wide, narrow, narrow),
        in_specs=[SMEM] + [VMEM] * 7, out_specs=(VMEM,) * 4, compiler_params=params(),
        name="prepare",
    )(side, factor, mix, *[jnp.asarray(v) for v in row_constants()])


def signed(ref_value):
    return 2.0 * ref_value.astype(F32) - 1.0


def store_edges(tile, top, bottom, p):
    for b in range(BANDS):
        top[p, b * HALF:(b + 1) * HALF, :] = tile[b, 0:HALF, :]
        bottom[p, b * HALF:(b + 1) * HALF, :] = tile[b, ROWS - HALF:ROWS, :]


def store_by_side(tile, lower, inner, outer, p):
    @pl.when(lower)
    def _():
        store_edges(tile, outer, inner, p)

    @pl.when(jnp.logical_not(lower))
    def _():
        store_edges(tile, inner, outer, p)


def edge_kernel(side, signs, scale, inner, outer):
    for p in range(signs.shape[0]):
        store_by_side(scale[...] * signed(signs[p]), side[0] == 0, inner, outer, p)


def edges(side, signs, scale):
    count = signs.shape[0]
    shape = jax.ShapeDtypeStruct((count, BANDS * HALF, COLS), F32)
    return pl.pallas_call(
        edge_kernel, grid=(count // PER,), out_shape=(shape, shape),
        in_specs=[
            SMEM,
            pl.BlockSpec((PER, BANDS, ROWS, COLS), lambda i: (i, 0, 0, 0)),
            pl.BlockSpec((BANDS, ROWS, COLS), lambda i: (0, 0, 0)),
        ],
        out_specs=[pl.BlockSpec((PER, BANDS * HALF, COLS), lambda i: (i, 0, 0))] * 2,
        compiler_params=params(), cost_estimate=cost(1e6, count * 2**19), name="edges",
    )(side, signs, scale)


def store_packed(tile, lower, near, far, p):
    lane = lax.broadcasted_iota(jnp.int32, (ROWS, 128), 1) // 16
    low = tile[0, :, :128]
    high = pltpu.roll(tile[0, :, 128:], 16, 1)
    for b in range(1, BANDS):
        low = jnp.where(lane == b, pltpu.roll(tile[b, :, :128], 16 * b, 1), low)
        mine = tile[b, :, 128:]
        if b < BANDS - 1:
            mine = pltpu.roll(mine, 16 * b + 16, 1)
        high = jnp.where(lane == b, mine, high)
    near[p] = jnp.where(lower, high, low)
    far[p] = jnp.where(lower, low, high)


def halo_rows(outer, inner, p):
    return jnp.concatenate([outer[p], inner[p], jnp.zeros((16, COLS), F32)], axis=0)


def first_kernel(side, signs, scale, inner, outer, matrix, out, near, far, after):
    hand_on(side, after)

    @pl.loop(0, out.shape[0], step=PER)
    def _(start):
        for p in range(PER):
            scaled = (scale[...] * signed(signs[start + p])).reshape(256, COLS)
            whole = jnp.concatenate([stacked(scaled), stacked(halo_rows(outer, inner, start + p))], axis=0)
            tile = dot(matrix[...], whole).reshape(BANDS, ROWS, COLS)
            out[start + p] = tile
            store_packed(tile, side[1] == 0, near, far, start + p)


def first_stage(side, signs, scale, inner, outer, matrix):
    count = signs.shape[0]
    packed = jax.ShapeDtypeStruct((count, ROWS, 128), F32)
    return pl.pallas_call(
        first_kernel,
        out_shape=(jax.ShapeDtypeStruct((count, BANDS, ROWS, COLS), F32), packed, packed, SIDE),
        in_specs=[SMEM] + [VMEM] * 5, out_specs=(VMEM, VMEM, VMEM, SMEM),
        compiler_params=params(), cost_estimate=cost(count * 2 * 256 * 1536 * 256, count * 2**20),
        name="first_stage",
    )(side, signs, scale, inner, outer, matrix)


def column_blur(lower, tiles, near, far, table, out):
    count = tiles.shape[0]
    flat = count * ROWS
    first = near[...].reshape(flat, 128)
    other = far[...].reshape(flat, 128)
    left = jnp.where(lower, other, first)
    right = jnp.where(lower, first, other)
    lane = lax.broadcasted_iota(jnp.int32, (flat, 128), 1)

    @pl.loop(0, BANDS, step=4)
    def _(start):
        for b in [start + j for j in range(4)]:
            uh, ul = split(tiles[:, b].reshape(flat, COLS))
            sides = jnp.where(lane < 16, pltpu.roll(left, 128 - 16 * b, 1), pltpu.roll(right, (144 - 16 * b) % 128, 1))
            sides = jnp.where(lane < 32, sides, pltpu.roll(sides, 32, 1))
            eh, el = split(sides)
            blurred = dot(jnp.concatenate([uh, ul, uh, eh, el], axis=1), table[b])
            out[:, b] = blurred.reshape(count, ROWS, COLS)


def middle_kernel(side, tiles, near, far, table, mix, back, weights, ahead, out, out_near, out_far, after, blurred):
    hand_on(side, after)
    lower = side[1] == 0
    column_blur(lower, tiles, near, far, table, blurred)
    weight = weights[...].reshape(256, COLS)

    group = 6 if tiles.shape[0] % 6 == 0 else 8

    @pl.loop(0, tiles.shape[0], step=group)
    def _(start):
        for p in range(group):
            weighted = weight * dot(mix[...], stacked(blurred[start + p].reshape(256, COLS)))
            tile = dot(back[...], stacked(weighted)).reshape(BANDS, ROWS, COLS)
            out[start + p] = tile
            store_packed(tile, lower, out_near, out_far, start + p)


def middle_stage(side, tiles, near, far, table, mix, back, weights, ahead):
    ahead = side if ahead is None else ahead
    count = tiles.shape[0]
    whole = jax.ShapeDtypeStruct((count, BANDS, ROWS, COLS), F32)
    packed = jax.ShapeDtypeStruct((count, ROWS, 128), F32)
    return pl.pallas_call(
        middle_kernel, out_shape=(whole, packed, packed, SIDE),
        in_specs=[SMEM] + [VMEM] * 7 + [pl.BlockSpec(memory_space=pl.ANY)], out_specs=(VMEM, VMEM, VMEM, SMEM),
        scratch_shapes=[pltpu.VMEM((count, BANDS, ROWS, COLS), F32)],
        compiler_params=params(), cost_estimate=cost(count * 10 * 2 * 256**3, count * 2**20),
        name="middle_stage",
    )(side, tiles, near, far, table, mix, back, weights, ahead)


def last_column_kernel(side, tiles, near, far, table, out, inner, outer, after):
    hand_on(side, after)
    column_blur(side[1] == 0, tiles, near, far, table, out)

    @pl.when(side[0] == 0)
    def _():
        @pl.loop(0, tiles.shape[0], step=PER)
        def _(start):
            for p in range(PER):
                store_edges(out[start + p], outer, inner, start + p)

    @pl.when(side[0] != 0)
    def _():
        @pl.loop(0, tiles.shape[0], step=PER)
        def _(start):
            for p in range(PER):
                store_edges(out[start + p], inner, outer, start + p)


def last_column_stage(side, tiles, near, far, table):
    count = tiles.shape[0]
    whole = jax.ShapeDtypeStruct((count, BANDS, ROWS, COLS), F32)
    edge = jax.ShapeDtypeStruct((count, BANDS * HALF, COLS), F32)
    return pl.pallas_call(
        last_column_kernel, out_shape=(whole, edge, edge, SIDE),
        in_specs=[SMEM] + [VMEM] * 4, out_specs=(VMEM, VMEM, VMEM, SMEM),
        compiler_params=params(), cost_estimate=cost(count * 4 * 2 * 256**3, count * 2**20),
        name="last_column_stage",
    )(side, tiles, near, far, table)


def sketch_kernel(side, tiles, inner, outer, matrix, signs, scale, out, after):
    hand_on(side, after)

    @pl.loop(0, out.shape[0], step=PER)
    def _(start):
        for p in range(PER):
            spot = start + p
            whole = jnp.concatenate(
                [stacked(tiles[spot].reshape(256, COLS)), stacked(halo_rows(outer, inner, spot))], axis=0
            )
            mixed = dot(matrix[...], whole).reshape(BANDS, ROWS, COLS)
            out[spot] = scale[...] * mixed + signed(signs[spot])


def sketch_stage(side, tiles, inner, outer, matrix, signs, scale):
    count = tiles.shape[0]
    return pl.pallas_call(
        sketch_kernel, out_shape=(jax.ShapeDtypeStruct((count, BANDS, ROWS, COLS), F32), SIDE),
        in_specs=[SMEM] + [VMEM] * 6, out_specs=(VMEM, SMEM),
        compiler_params=params(), cost_estimate=cost(count * 2 * 256 * 1536 * 256, count * 2**20),
        name="sketch_stage",
    )(side, tiles, inner, outer, matrix, signs, scale)


def sketch_main_kernel(side, tiles, matrix, out, after):
    hand_on(side, after)

    @pl.loop(0, out.shape[0], step=PER)
    def _(start):
        for p in range(PER):
            out[start + p] = dot(matrix[:, 0:768], stacked(tiles[start + p].reshape(256, COLS)))


def sketch_main_stage(side, tiles, matrix):
    count = tiles.shape[0]
    return pl.pallas_call(
        sketch_main_kernel, out_shape=(jax.ShapeDtypeStruct((count, 256, COLS), F32), SIDE),
        in_specs=[SMEM, VMEM, VMEM], out_specs=(VMEM, SMEM),
        compiler_params=params(), cost_estimate=cost(count * 256 * 1536 * 256, count * 2**19),
        name="sketch_main_stage",
    )(side, tiles, matrix)


def gather_group(refs, g):
    return jnp.concatenate([r[:, g].reshape(-1, COLS) for r in refs], axis=0)


def same_place(shape):
    return lax.broadcasted_iota(jnp.int32, shape, 0) % 8 == lax.broadcasted_iota(jnp.int32, shape, 1) % 8


def spread_ones(shape, long_dim):
    long = lax.broadcasted_iota(jnp.int32, shape, long_dim) // 8
    short = lax.broadcasted_iota(jnp.int32, shape, 1 - long_dim)
    return (long == short).astype(F32)


def collapse(table):
    kept = jnp.where(same_place(table.shape), table, 0.0)
    rows, cols = table.shape
    return dot(dot(spread_ones((rows // 8, rows), 1), kept, HI), spread_ones((cols, cols // 8), 0), HI)


def early_gram_kernel(side, *refs):
    chunks, out, after, even, cross = refs[:-4], refs[-4], refs[-3], refs[-2], refs[-1]
    hand_on(side, after)
    even[...] = jnp.zeros_like(even)
    cross[...] = jnp.zeros_like(cross)

    @pl.loop(0, chunks[0].shape[1], step=8)
    def _(g):
        values = jnp.concatenate([gather_group(chunks, g + j) for j in range(8)], axis=1)
        high, low = split(values)
        even[...] += dot_nt(high, high) + dot_nt(low, low)
        cross[...] += dot_nt(high, low)

    mixed = collapse(cross[...])
    out[...] = collapse(even[...]) + (mixed + mixed.T)


def early_gram_stage(side, chunks):
    probes = sum(c.shape[0] for c in chunks)
    return pl.pallas_call(
        early_gram_kernel, out_shape=(jax.ShapeDtypeStruct((probes, probes), F32), SIDE),
        in_specs=[SMEM] + [VMEM] * len(chunks), out_specs=(VMEM, SMEM),
        scratch_shapes=[pltpu.VMEM((8 * probes, 8 * probes), F32)] * 2,
        compiler_params=params(), cost_estimate=cost(32 * 2 * 2 * 256**3, 2**23), name="early_gram_stage",
    )(side, *chunks)


def gram_kernel(early, main, inner, outer, matrix, signs, scale, *refs):
    chunks, out, sketch, total = refs[:-3], refs[-3], refs[-2], refs[-1]
    total[...] = jnp.zeros_like(total)
    done = early.shape[0]

    @pl.loop(0, main.shape[0], step=PER)
    def _(start):
        for p in range(PER):
            spot = start + p
            mixed = main[spot] + dot(matrix[:, 768:], stacked(halo_rows(outer, inner, spot)))
            values = scale[...] * mixed.reshape(BANDS, ROWS, COLS) + signed(signs[spot])
            sketch[spot] = values.reshape(BANDS * ROWS // 8, 8, COLS)

    whole = chunks + (sketch,)

    @pl.loop(0, sketch.shape[1], step=8)
    def _(g):
        values = jnp.concatenate([gather_group(whole, g + j) for j in range(8)], axis=1)
        high, low = split(values)
        new_high, new_low = high[8 * done:], low[8 * done:]
        total[...] += dot_nt(jnp.concatenate([new_high, new_low], axis=0), high)
        total[...] += dot_nt(jnp.concatenate([new_low, new_high], axis=0), low)

    rows = total.shape[0] // 2
    late = collapse(total[0:rows] + total[rows:])
    corner = 0.5 * (late[:, done:] + late[:, done:].T)
    gram = jnp.concatenate(
        [
            jnp.concatenate([early[...], late[:, :done].T], axis=1),
            jnp.concatenate([late[:, :done], corner], axis=1),
        ],
        axis=0,
    )
    out[0] = jnp.concatenate([gram[8 * j:8 * j + 8] for j in range(4)], axis=1)
    out[1] = jnp.zeros(out.shape[1:], F32)


def gram_stage(early, main, inner, outer, matrix, signs, scale, chunks):
    count = main.shape[0]
    probes = sum(c.shape[0] for c in chunks) + count
    grouped = jax.ShapeDtypeStruct((count, BANDS * ROWS // 8, 8, COLS), F32)
    return pl.pallas_call(
        gram_kernel, out_shape=(jax.ShapeDtypeStruct((2, 8, 128), F32), grouped),
        in_specs=[VMEM] * (7 + len(chunks)), out_specs=(VMEM, VMEM),
        scratch_shapes=[pltpu.VMEM((16 * count, 8 * probes), F32)],
        compiler_params=params(), cost_estimate=cost(32 * 2 * 2 * 256**3, 2**23), name="gram_stage",
    )(early, main, inner, outer, matrix, signs, scale, *chunks)


def group_blocks(chunks):
    return [pl.BlockSpec((c.shape[0], PER, 8, COLS), lambda i: (0, i, 0, 0)) for c in chunks]


def two_sum(a, b):
    total = a + b
    part = total - a
    return total, (a - (total - part)) + (b - part)


def quick_sum(a, b):
    total = a + b
    return total, b - (total - a)


def halves(a):
    wide = a * 4097.0
    high = wide - (wide - a)
    return high, a - high


def two_product(a, b):
    product = a * b
    ah, al = halves(a)
    bh, bl = halves(b)
    return product, ((ah * bh - product) + ah * bl + al * bh) + al * bl


def pair_add(a, b):
    total, error = two_sum(a[0], b[0])
    return quick_sum(total, error + (a[1] + b[1]))


def pair_mul(a, b):
    product, error = two_product(a[0], b[0])
    return quick_sum(product, error + (a[0] * b[1] + a[1] * b[0]))


def pair_neg(a):
    return -a[0], -a[1]


def merge_kernel(mine, other, out):
    total = pair_add((mine[0], mine[1]), (other[0], other[1]))
    out[0] = total[0]
    out[1] = total[1]


def merge(mine, other):
    return pl.pallas_call(
        merge_kernel, out_shape=jax.ShapeDtypeStruct(mine.shape, F32),
        in_specs=[VMEM] * 2, out_specs=VMEM, compiler_params=params(), name="merge",
    )(mine, other)


def sum_over(value, axis):
    count = lax.axis_size(axis)
    bit = 1
    while bit < count:
        value = merge(value, lax.ppermute(value, axis, [(i, i ^ bit) for i in range(count)]))
        bit *= 2
    return value


def factor_kernel(gram, factor, inverse, work, *, norm):
    order = factor.shape[0]
    work[...] = jnp.zeros_like(work)
    row = lax.broadcasted_iota(jnp.int32, (order, 128), 0)
    lane = lax.broadcasted_iota(jnp.int32, (order, 128), 1)
    work[0] = (lane == row + order).astype(F32)
    for j in range(4):
        work[:, 8 * j:8 * j + 8, 0:order] = gram[:, :, j * order:(j + 1) * order]
    now = (work[0], work[1])
    finished, base, place = [], 0, row
    for k in range(order - 1):
        if k - base == 8:
            finished.append(now[0][:8])
            now = tuple(v[8:] for v in now)
            base, place = k, place[8:]
        pivot_row = tuple(v[k - base:k - base + 1, :] for v in now)
        pivot = tuple(jnp.broadcast_to(v[:, k:k + 1], (1, 128)) for v in pivot_row)
        first = pivot_row[0] / pivot[0]
        rest = pair_add(pivot_row, pair_neg(pair_mul((first, jnp.zeros_like(first)), pivot)))
        ratio = quick_sum(first, rest[0] / pivot[0])
        column = tuple(
            jnp.where(place > k, jnp.broadcast_to(v[:, k:k + 1], (order - base, 128)), 0.0) for v in now
        )
        now = pair_add(now, pair_neg(pair_mul(column, ratio)))
    reduced = jnp.concatenate(finished + [now[0]], axis=0)
    diagonal = jnp.sum(jnp.where(lane == row, reduced, 0.0), axis=1, keepdims=True)
    scaled = reduced / jnp.sqrt(diagonal)
    factor[...] = jnp.where(lane >= row, scaled, 0.0)[:, 0:order] * (1.0 / norm)
    inverse[...] = scaled[:, order:2 * order] * norm


def factor_stage(gram, order, norm):
    square = jax.ShapeDtypeStruct((order, order), F32)
    return pl.pallas_call(
        lambda *refs: factor_kernel(*refs, norm=norm), out_shape=(square, square),
        in_specs=[VMEM], out_specs=(VMEM, VMEM), scratch_shapes=[pltpu.VMEM((2, order, 128), F32)],
        compiler_params=params(), name="factor_stage",
    )(gram)


def basis_kernel(inverse, *refs):
    chunks, out, matrix = refs[:-2], refs[-2], refs[-1]
    order = matrix.shape[0]

    @pl.when(pl.program_id(0) == 0)
    def _():
        wide = dot(dot(spread_ones((order, order // 8), 0), inverse[...], HI), spread_ones((order // 8, order), 1), HI)
        high, low = split(jnp.where(same_place((order, order)), wide, 0.0))
        matrix[:, 0:order] = high
        matrix[:, order:2 * order] = low
        matrix[:, 2 * order:3 * order] = high

    start = pl.program_id(0) * out.shape[1]
    for g in range(out.shape[1]):
        values = dot(matrix[...], stacked(gather_group(chunks, start + g)))
        out[:, g] = values.reshape(-1, 8, COLS)


def basis_stage(inverse, chunks):
    probes = inverse.shape[0]
    groups = chunks[0].shape[1]
    return pl.pallas_call(
        basis_kernel, grid=(groups // 8,),
        out_shape=jax.ShapeDtypeStruct((probes, groups, 8, COLS), F32),
        in_specs=[VMEM] * (1 + len(chunks)),
        out_specs=pl.BlockSpec((probes, 8, 8, COLS), lambda i: (0, i, 0, 0)),
        scratch_shapes=[pltpu.VMEM((256, 768), BF16)],
        compiler_params=params(), cost_estimate=cost(32 * 3 * 2 * 256**3, 2**24), name="basis_stage",
    )(inverse, *chunks)


def swap(inner, outer, axis):
    count = lax.axis_size(axis)
    pairs = [(i, i ^ 1) for i in range(count)]
    others = [p for i in range(1, count - 1, 2) for p in ((i, i + 1), (i + 1, i))]
    return lax.ppermute(inner, axis, pairs), lax.ppermute(outer, axis, others)


def shards(probe_signs, prior_scale, prior_factor, band_mix, inverse_noise_variance):
    probes = probe_signs.shape[0]
    side = jnp.stack([lax.axis_index("row") % 2, lax.axis_index("col") % 2]).astype(jnp.int32)
    table = jnp.asarray(col_constants())
    starts = [sum(CHUNKS[:k]) for k in range(len(CHUNKS))]
    signs = [probe_signs[start:start + count] for start, count in zip(starts, CHUNKS)]
    rows = [swap(*edges(side, part, prior_scale), "row") for part in signs]
    first_m, last_m, mix_m, back_m = prepare(side, prior_factor, band_mix)
    last = len(CHUNKS) - 1
    state = {}

    def first(k, side):
        *state[k], side = first_stage(side, signs[k], prior_scale, *rows[k], first_m)
        state[k][1:] = swap(*state[k][1:], "col")
        return side

    def middle(k, side, ahead=None):
        *state[k], side = middle_stage(side, *state[k], table, mix_m, back_m, inverse_noise_variance, ahead)
        state[k][1:] = swap(*state[k][1:], "col")
        return side

    def last_column(k, side):
        *state[k], side = last_column_stage(side, *state[k], table)
        state[k][1:] = swap(*state[k][1:], "row")
        return side

    def finish(k, side):
        state[k], side = sketch_stage(side, *state[k], last_m, signs[k], prior_scale)
        return side

    def group(k):
        return state[k].reshape(CHUNKS[k], BANDS * ROWS // 8, 8, COLS)

    side = first(0, side)
    side = middle(0, side)
    side = first(1, side)
    side = last_column(0, side)
    for k in range(2, last + 1):
        side = middle(k - 1, side, state[k - 2][1])
        side = first(k, side)
        side = last_column(k - 1, side)
    side = middle(last, side, state[last - 1][1])
    for k in range(last - 1):
        side = finish(k, side)
    side = last_column(last, side)
    side = finish(last - 1, side)
    grouped = [group(k) for k in range(last)]
    early, side = early_gram_stage(side, grouped)
    tiles, *edge_rows = state[last]
    main, side = sketch_main_stage(side, tiles, last_m)
    gram, latest = gram_stage(early, main, *edge_rows, last_m, signs[last], prior_scale, grouped)
    grouped.append(latest)
    gram = sum_over(sum_over(gram, "row"), "col")
    total = BANDS * ROWS * COLS * lax.axis_size("row") * lax.axis_size("col")
    r_factor, inverse = factor_stage(gram, probes, float(np.sqrt(np.float32(total))))
    basis = basis_stage(inverse, grouped)
    return basis.reshape(probes, BANDS, ROWS, COLS), r_factor


def solution(mesh):
    in_specs = (P(None, None, "row", "col"), P(None, "row", "col"), P(), P(), P(None, "row", "col"))
    out_specs = (P(None, None, "row", "col"), P())
    return jax.shard_map(shards, mesh=mesh, in_specs=in_specs, out_specs=out_specs, check_vma=False)
```
